512 devices in a mesh: lat: 64 (over z_hi, y, core), wave: 8 (over x, z_lo).
Axes of the slice: x: 4, y: 8, z: 8 (z_hi: 4, z_lo: 2; z = z_hi * 2 + z_lo), core: 2. Of those that a mesh axis runs over, the one named last changes fastest.
Arguments:
- grid_field: float32 [16, 512, 768], P('wave', 'lat'), may hold values from -6 to 6
- row_longitudes: int32 [512], P('lat'), may hold values from 96 to 768, as said below
- owner_order: int32 [384], replicated, may hold values from 0 to 383, each once
- legendre: float32 [512, 384, 384], P('lat'), may hold values from -0.75 to 0.75
- vertical_band: float32 [4, 3, 4], replicated, may hold values from -1.5 to 1.5
Outputs:
- spectral: float32 [384, 384, 2, 16], P('lat', 'wave')
The draws below stay inside these ranges and needn't reach their ends.
Inputs may be any that keep to these rules, and one draw needn't show every extreme that they name: `row_longitudes`: at least one row has all 768 longitudes. `owner_order`: each zonal wavenumber appears once; wave device g owns the slots g * 384 // 8 onward.
All inputs are finite; a program needn't handle non-finite values.
Results may differ from the reference program's by a relative error of at most 0.0003.
Values sent between devices are 32-bit elements; how exact they have to be, the bound alone decides.
A program may use at most 128 MiB of HBM per device.

```python
import math
import jax
import jax.numpy as jnp
from jax import lax

MW = 384
NLON = 768
FIELDS = 4
LEVELS = 4
NN = 384
LAYERS = 16
ROWS = 512


def draw_row_longitudes(key, part):
    raw_points = jax.random.randint(key, (ROWS,), NLON // 8, NLON + NLON // 4 + 1)
    return jnp.minimum(raw_points, NLON).astype(jnp.int32)


def with_spikes(array, own_key, source, target, parts, factor):
    owner, partner = [(jnp.arange(array.shape[dim]) // (array.shape[dim] // parts)).reshape([-1 if axis == dim else 1 for axis in range(array.ndim)]) for dim in (source, target)]
    chosen = jax.random.permutation(own_key, parts)[partner]
    strong = (owner == chosen) | (owner == (partner + parts // 2) % parts)
    return jnp.where(strong, factor * array, array)


def block_scale(own_key, extent, shards, smallest, top_value):
    gain = 1.0
    for axis_at, parts in shards:
        draws = jax.random.uniform(jax.random.fold_in(jax.random.fold_in(own_key, 6), axis_at), (parts,), jnp.float32, smallest / len(shards), top_value / len(shards))
        gain = gain * jnp.repeat(jnp.exp(draws), extent[axis_at] // parts).reshape((-1,) + (1,) * (len(extent) - 1 - axis_at))
    return gain


def normal_values(rng, shape, spread, bound, split=(), held_as=jnp.bfloat16):
    drawn = jax.random.normal(rng, shape, jnp.float32) * spread
    if len(split) > 0:
        drawn = block_scale(rng, shape, split, -0.22, 0.18) * drawn
    return jnp.clip(drawn, min=-bound, max=bound).astype(held_as)


def noise_with(own_key, dims, spread, limit, pieces, heavy, kind=jnp.bfloat16):
    drawn = spread * jax.random.normal(own_key, dims, jnp.float32)
    if pieces:
        drawn = drawn * block_scale(own_key, dims, pieces, -0.22, 0.18)
    return jnp.clip(with_spikes(drawn, jax.random.fold_in(own_key, 3), *heavy), -limit, limit).astype(kind)


def setup_inputs(seed: int = 0) -> dict:
    splits = jax.random.split(jax.random.key(seed), 6)
    grid_field = normal_values(splits[0], (LAYERS, ROWS, NLON), 1.0, 6.0, ((0, 8), (1, 64)), jnp.float32)
    row_longitudes = draw_row_longitudes(jax.random.fold_in(splits[5], 71), 0)
    owner_order = jax.random.permutation(splits[2], MW).astype(jnp.int32)
    legendre = noise_with(splits[3], (ROWS, MW, NN), ROWS ** -0.5, 0.75, ((0, 64),), (0, 2, 64, 4.0), jnp.float32)
    vertical_band = jnp.clip(jax.random.uniform(splits[4], (FIELDS, 3, LEVELS), jnp.float32, -1.5, 1.5), -1.5, 1.5)
    return {"grid_field": grid_field, "row_longitudes": row_longitudes, "owner_order": owner_order, "legendre": legendre, "vertical_band": vertical_band}


def row_fourier(wavenumbers, row_values, row_points):
    columns = jnp.arange(NLON, dtype=jnp.int32)
    phase_steps = wavenumbers[None, :] * columns[:, None] % row_points
    phases = phase_steps.astype(jnp.float32) * (2.0 * math.pi / row_points.astype(jnp.float32))
    active = (columns[:, None] < row_points) & (2 * wavenumbers[None, :] < row_points)
    norm_factor = 1.0 / jnp.sqrt(row_points.astype(jnp.float32))
    cosine = jnp.where(active, jnp.cos(phases), 0.0) * norm_factor
    sine_part = jnp.where(active, -jnp.sin(phases), 0.0) * norm_factor
    transform = jnp.concatenate([cosine, sine_part], axis=1)
    return jnp.dot(row_values, transform, precision=lax.Precision.HIGHEST, preferred_element_type=jnp.float32)

def vertical(sums, vertical_band, degrees):
    components = sums.reshape(sums.shape[:3] + (FIELDS, LEVELS))
    sub_diagonal = vertical_band[:, 0, :]
    main_diagonal = vertical_band[:, 1, :]
    super_diagonal = vertical_band[:, 2, :]
    zero_level = jnp.zeros_like(components[..., :1])
    level_below = jnp.concatenate([zero_level, components[..., :-1]], axis=-1)
    level_above = jnp.concatenate([components[..., 1:], zero_level], axis=-1)
    coupled = sub_diagonal * level_below + main_diagonal * components + super_diagonal * level_above
    laplace_ratio = (degrees * (degrees + 1.0) / (MW * MW)).reshape(-1, 1, 1, 1, 1)
    return (components + laplace_ratio * coupled).reshape(sums.shape)

def reference(grid_field, row_longitudes, owner_order, legendre, vertical_band):

    def one_row(pair):
        return row_fourier(owner_order, pair[0], pair[1])
    fourier = lax.map(one_row, (jnp.moveaxis(grid_field, 1, 0), row_longitudes))
    fourier = fourier.reshape(ROWS, LAYERS, 2, MW)
    degree_ids = jnp.arange(NN, dtype=jnp.int32)
    triangle = degree_ids[None, :] >= owner_order[:, None]
    chosen = jnp.where(triangle[None], jnp.take(legendre, owner_order, axis=1), 0.0)
    sums = jnp.einsum('rkn,rlck->nkcl', chosen, fourier, precision=lax.Precision.HIGHEST)
    degrees = degree_ids.astype(jnp.float32)
    return vertical(sums, vertical_band, degrees)
```

```python
import functools

import jax
import jax.numpy as jnp
from jax import lax
from jax.experimental import pallas as pl
from jax.experimental.pallas import tpu as pltpu
from jax.sharding import PartitionSpec as P

MESH = pl.DeviceIdType.MESH
F32 = jnp.float32
BF16 = jnp.bfloat16

MW = 384
NN = 384
NLON = 768
FIELDS = 4
LEVELS = 4
LAYERS = 16
ZH = 4
NY = 8
NX = 4
ZL = 2
R = 8
KW = 48
NI = 6
NB = 128
NA = NLON // NB
JA = 8
JB = 4

COS = (1.0, -19.739208221435547, 64.93939208984375, -85.45665740966797, 60.242130279541016, -26.4046688079834,
       7.800131320953369, -1.4531123638153076)
SIN = (6.2831854820251465, -41.34170150756836, 81.6052474975586, -76.70580291748047, 42.05775451660156,
       -15.086565017700195, 3.7813189029693604, -0.6207788586616516)


def iota(shape, dim):
    return lax.broadcasted_iota(jnp.int32, shape, dim)


def split(x):
    hi = x.astype(BF16)
    return hi, (x - hi.astype(F32)).astype(BF16)


def nt(a, b):
    return lax.dot_general(a, b, (((1,), (1,)), ((), ())), preferred_element_type=F32)


def nn(a, b):
    return jnp.dot(a, b, preferred_element_type=F32)


def polynomial(coefficients, u):
    total = jnp.full_like(u, coefficients[-1])
    for c in coefficients[-2::-1]:
        total = total * u + c
    return total


def cos_sin(steps, points, inverse):
    turns = (steps - jnp.floor(steps * inverse + 0.5) * points) * inverse
    u = turns * turns
    return polynomial(COS, u), polynomial(SIN, u) * turns


def halves(extent):
    steps = []
    for s in range(extent // 2):
        for direction in (0, 1):
            for h in (0, 1):
                first = 0 if h == direction else 1
                if s >= first:
                    steps.append((direction, s, h, s > first))
    return steps


def kernel(
    grid_ref, lon_ref, order_ref, leg_ref, band_ref, out_ref,
    leg_v, gath, gx, e_s, tw_s, ft, xs, ra, rb, core_a, core_b, ring_a, ring_b, half_a, half_b,
    leg_sem, own_sem, g_send, g_recv, ca_send, ca_recv, cb_send, cb_recv,
    ra_send, ra_recv, rb_send, rb_recv, da_send, da_recv, db_send, db_recv,
):
    lw = LAYERS // (NX * ZL)
    lat, wave = lax.axis_index("lat"), lax.axis_index("wave")
    core = lax.rem(lat, 2)
    y = lax.rem(lat // 2, NY)
    zh = lat // (2 * NY)
    x = wave // ZL
    zl = lax.rem(wave, ZL)

    def at_y(o):
        return ((zh * NY + lax.rem(y + o + NY, NY)) * 2 + core, wave)

    def at_z(o):
        return ((lax.rem(zh + o + ZH, ZH) * NY + y) * 2 + core, wave)

    def at_w(dx, dz):
        return (lat, lax.rem(x + dx, NX) * ZL + lax.rem(zl + dz, ZL))

    sibling = (lat + 1 - 2 * core, wave)
    wave_peers = [(dx, dz) for dx in range(NX) for dz in range(ZL) if (dx, dz) != (0, 0)]

    leg_copies = []
    for t in range(NN // NB):
        copy = pltpu.make_async_copy(leg_ref.at[:, t * NB : (t + 1) * NB], leg_v.at[t], leg_sem.at[t])
        copy.start()
        leg_copies.append(copy)
    mine = pl.ds(pl.multiple_of(wave * (lw * R), 8), lw * R)
    own_copy = pltpu.make_async_copy(grid_ref, gath.at[mine], own_sem)
    own_copy.start()

    barrier = pltpu.get_barrier_semaphore()
    peers = [at_w(dx, dz) for dx, dz in wave_peers] + [sibling]
    peers += [at_y(o) for o in range(1, NY)] + [at_z(o) for o in range(1, ZH)]
    for peer in peers:
        pl.semaphore_signal(barrier, inc=1, device_id=peer, device_id_type=MESH)
    pl.semaphore_wait(barrier, len(peers))

    def remote(src, dst, send, recv, peer):
        copy = pltpu.make_async_remote_copy(
            src_ref=src, dst_ref=dst, send_sem=send, recv_sem=recv, device_id=peer, device_id_type=MESH
        )
        return copy

    grid_copies = []
    for i, (dx, dz) in enumerate(wave_peers):
        copy = remote(grid_ref, gath.at[mine], g_send.at[i], g_recv.at[i], at_w(dx, dz))
        copy.start()
        grid_copies.append(copy)

    sub = iota((8, NB), 0)
    waves = []
    for t in range(KW // 8):
        column = jnp.zeros((8, NB), F32)
        for s in range(8):
            column = jnp.where(sub == s, order_ref[wave * KW + t * 8 + s].astype(F32), column)
        waves.append(column)
    waves = jnp.concatenate(waves, axis=0)

    lane = iota((KW, NB), 1)
    low = lane.astype(F32)
    high = ((lane // LAYERS) * NB).astype(F32)
    for r in range(R):
        points = jnp.full((KW, NB), lon_ref[r], jnp.int32).astype(F32)
        inverse = 1.0 / points
        cos_low, sin_low = cos_sin(waves * low, points, inverse)
        table_hi, table_lo = split(jnp.concatenate([cos_low, -sin_low], axis=0))
        e_s[r * 2 * KW : (r + 1) * 2 * KW, :] = jnp.concatenate([table_hi, table_hi, table_lo], axis=1)
        cos_high, sin_high = cos_sin(waves * high, points, inverse)
        factor = jnp.where(2.0 * waves < points, 1.0 / jnp.sqrt(points), 0.0)
        tw_s[r * 2 * KW : r * 2 * KW + KW, :] = cos_high * factor
        tw_s[r * 2 * KW + KW : (r + 1) * 2 * KW, :] = -sin_high * factor

    n_lane = iota((1, NN), 1).astype(F32) + 0.5
    z_of = jnp.floor(n_lane * (1.0 / (NI * 2 * NY)))
    rest = n_lane - z_of * (NI * 2 * NY)
    y_of = jnp.floor(rest * (1.0 / (NI * 2)))
    rest = rest - y_of * (NI * 2)
    c_of = jnp.floor(rest * (1.0 / NI))
    i_of = rest - c_of * NI - 0.5
    z_rel = z_of - zh.astype(F32)
    z_rel = jnp.where(z_rel < 0, z_rel + ZH, z_rel)
    y_rel = y_of - y.astype(F32)
    y_rel = jnp.where(y_rel < 0, y_rel + NY, y_rel)
    c_rel = jnp.where(c_of == core.astype(F32), 0.0, 1.0)
    n_row = iota((NN, NN), 0).astype(F32)
    place_a = ((c_rel * NY + y_rel) * ZH + z_rel) * NI + i_of
    place_b = ((c_rel * ZH + z_rel) * NY + y_rel) * NI + i_of
    order_a = jnp.where(n_row == place_a, 1.0, 0.0).astype(BF16)
    order_b = jnp.where(n_row == place_b, 1.0, 0.0).astype(BF16)

    def slot(g, q):
        return (q % 4) * (KW // 4) + 2 * g + q // 4

    groups = KW // 8
    for copy in leg_copies:
        copy.wait()
    n_of = iota((R, NN), 1)
    for g in range(groups):
        rows = []
        for q in range(8):
            m = order_ref[wave * KW + slot(g, q)]
            picked = jnp.concatenate([leg_v[t, pl.ds(m, R, stride=MW), :] for t in range(NN // NB)], axis=1)
            rows.append(jnp.where(n_of >= m, picked, 0.0))
        hi, lo = split(jnp.concatenate(rows, axis=0))
        turned = nt(order_a if 2 * g < JA else order_b, jnp.concatenate([hi, lo], axis=0))
        xs[g] = turned.astype(BF16)

    own_copy.wait()
    for copy in grid_copies:
        copy.wait_recv()
    for layer in range(LAYERS):
        for a in range(NA):
            gx[a, pl.ds(layer, R, stride=LAYERS), :] = gath[layer * R : (layer + 1) * R, a * NB : (a + 1) * NB]

    spread = jnp.where(iota((2 * NB, NB), 0) % LAYERS == iota((2 * NB, NB), 1) % LAYERS, 1.0, 0.0).astype(BF16)
    column = iota((LAYERS, NB), 1)
    for r in range(R):
        points = lon_ref[r]
        parts = [
            jnp.where(column + a * NB < points, gx[a, r * LAYERS : (r + 1) * LAYERS, :], 0.0) for a in range(NA)
        ]
        parts += [jnp.zeros((LAYERS, NB), F32)] * (NB // LAYERS - NA)
        hi, lo = split(jnp.concatenate(parts, axis=0))
        first = nt(e_s[r * 2 * KW : (r + 1) * 2 * KW, :], jnp.concatenate([hi, lo, hi], axis=1))
        re, im = first[:KW], first[KW:]
        tw_re = tw_s[r * 2 * KW : r * 2 * KW + KW, :]
        tw_im = tw_s[r * 2 * KW + KW : (r + 1) * 2 * KW, :]
        both = jnp.concatenate([re * tw_re - im * tw_im, re * tw_im + im * tw_re], axis=0)
        hi, lo = split(both)
        ft[r * 2 * KW : (r + 1) * 2 * KW, :] = nn(jnp.concatenate([hi, lo], axis=1), spread)

    lanes = iota((R, NB), 1)
    k4_of = lanes // (2 * LAYERS)
    is_cos = (lanes // LAYERS) % 2 == 0
    diagonals = []
    for g in range(groups):
        rows = []
        for q in range(8):
            k = slot(g, q)
            value = jnp.where(is_cos, ft[pl.ds(k, R, stride=2 * KW), :], ft[pl.ds(KW + k, R, stride=2 * KW), :])
            value = jnp.where(k4_of == q % 4, value, 0.0)
            zero = jnp.zeros((R, NB), F32)
            rows.append(jnp.concatenate([value, zero] if q < 4 else [zero, value], axis=1))
        hi, lo = split(jnp.concatenate(rows, axis=0))
        diagonals.append(jnp.concatenate([hi, hi, lo, lo], axis=0))

    half_n = NN // 2

    def partial_sums(c):
        for g in range(groups):
            turned = xs[g, c * half_n : (c + 1) * half_n, :]
            sums = nn(jnp.concatenate([turned, turned], axis=1), diagonals[g])
            for t in (0, 1):
                j = 2 * g + t
                value = sums[:, t * NB : (t + 1) * NB]
                if j < JA:
                    ra[pl.ds(c * half_n * JA + j, half_n, stride=JA), :] = value
                else:
                    rb[pl.ds(c * half_n * JB + j - JA, half_n, stride=JB), :] = value

    part_a = ZH * NI * JA
    part_b = NY * NI * JB
    y_order = sorted(range(NY), key=lambda o: -min(o, NY - o))
    z_order = sorted(range(ZH), key=lambda o: -min(o, ZH - o))

    partial_sums(1)
    core_copies = []
    copies_a, copies_b = {}, {}
    for at in range(max(NY, ZH)):
        if at < NY:
            o = y_order[at]
            copies_a[o] = remote(
                ra.at[pl.ds(half_n * JA + o * part_a, part_a)], core_a.at[pl.ds(o * part_a, part_a)],
                ca_send.at[o], ca_recv.at[o], sibling,
            )
            copies_a[o].start()
        if at < ZH:
            o = z_order[at]
            copies_b[o] = remote(
                rb.at[pl.ds(half_n * JB + o * part_b, part_b)], core_b.at[pl.ds(o * part_b, part_b)],
                cb_send.at[o], cb_recv.at[o], sibling,
            )
            copies_b[o].start()
    partial_sums(0)

    ha, hb = part_a // 2, part_b // 2
    started = []
    done_a, done_b = set(), set()

    def own_part(o, own, from_core, copies, done, part):
        if o not in done:
            copies[o].wait_recv()
            done.add(o)
            rows = pl.ds(o * part, part)
            own[rows, :] = own[rows, :] + from_core[rows, :]

    def ring_step(item, extent, own, from_core, copies, done, part, ring, send, recv, at, pending):
        direction, s, h, has = item
        o = extent // 2 - s if direction == 0 else extent // 2 + s
        own_part(o, own, from_core, copies, done, part)
        rows = pl.ds(o * part + h * (part // 2), part // 2)
        if has:
            pending[(direction, s - 1, h)].wait_recv()
            own[rows, :] = own[rows, :] + ring[direction, s - 1, h]
        copy = remote(
            own.at[rows], ring.at[direction, s, h], send.at[direction, s, h], recv.at[direction, s, h],
            at(1 if direction == 0 else -1),
        )
        copy.start()
        pending[(direction, s, h)] = copy

    def ring_end(extent, own, from_core, copies, done, part, ring, pending, h):
        own_part(0, own, from_core, copies, done, part)
        rows = pl.ds(h * (part // 2), part // 2)
        total = own[rows, :]
        for direction in (0, 1):
            last = (direction, extent // 2 - 1, h)
            if last in pending:
                pending[last].wait_recv()
                total = total + ring[direction, extent // 2 - 1, h]
        own[rows, :] = total

    pend_a, pend_b = {}, {}
    args_a = (NY, ra, core_a, copies_a, done_a, part_a, ring_a)
    args_b = (ZH, rb, core_b, copies_b, done_b, part_b, ring_b)
    for s in range(max(NY, ZH) // 2):
        for item in halves(NY):
            if item[1] == s:
                ring_step(item, *args_a, ra_send, ra_recv, at_y, pend_a)
        for item in halves(ZH):
            if item[1] == s:
                ring_step(item, *args_b, rb_send, rb_recv, at_z, pend_b)

    for h in (0, 1):
        ring_end(*args_b, pend_b, h)
    rows_b = NI * JB
    direct_b = []
    for o in range(1, NY):
        copy = remote(
            rb.at[pl.ds(o * rows_b, rows_b)], half_b.at[pl.ds((o - 1) * rows_b, rows_b)],
            db_send.at[o - 1], db_recv.at[o - 1], at_y(o),
        )
        copy.start()
        direct_b.append(copy)
    for h in (0, 1):
        ring_end(*args_a, pend_a, h)
    rows_a = NI * JA
    direct_a = []
    for o in range(1, ZH):
        copy = remote(
            ra.at[pl.ds(o * rows_a, rows_a)], half_a.at[pl.ds((o - 1) * rows_a, rows_a)],
            da_send.at[o - 1], da_recv.at[o - 1], at_z(o),
        )
        copy.start()
        direct_a.append(copy)

    band = [jnp.zeros((1, NB), F32) for _ in range(3)]
    layer_of = iota((1, NB), 1) % LAYERS
    for d in range(3):
        for f in range(FIELDS):
            for l in range(LEVELS):
                if (d, l) in ((0, 0), (2, LEVELS - 1)):
                    continue
                band[d] = jnp.where(layer_of == f * LEVELS + l, band_ref[d, f, l], band[d])

    def vertical(total, width):
        degree = iota(total.shape, 0) // width + lat * NI
        degree = degree.astype(F32)
        ratio = degree * (degree + 1.0) * (1.0 / (MW * MW))
        below = pltpu.roll(total, 1, 1)
        above = pltpu.roll(total, NB - 1, 1)
        return total + ratio * (band[0] * below + band[1] * total + band[2] * above)

    total_b = rb[:rows_b, :]
    for o in range(1, NY):
        direct_b[o - 1].wait_recv()
        total_b = total_b + half_b[(o - 1) * rows_b : o * rows_b, :]
    total_b = vertical(total_b, JB)
    total_a = ra[:rows_a, :]
    for o in range(1, ZH):
        direct_a[o - 1].wait_recv()
        total_a = total_a + half_a[(o - 1) * rows_a : o * rows_a, :]
    total_a = vertical(total_a, JA)

    fill = jnp.zeros((NB - rows_a - rows_b, NB), F32)
    turned = jnp.concatenate([total_a, total_b, fill], axis=0).T
    cl = 2 * LAYERS
    for i in range(NI):
        pieces = []
        for k4 in range(4):
            rows = turned[k4 * cl : (k4 + 1) * cl]
            pieces.append(rows[:, i * JA : (i + 1) * JA])
            pieces.append(rows[:, rows_a + i * JB : rows_a + (i + 1) * JB])
        out_ref[i] = jnp.concatenate(pieces, axis=1)

    sent = grid_copies + list(copies_a.values()) + list(copies_b.values()) + list(pend_a.values())
    for copy in sent + list(pend_b.values()) + direct_a + direct_b:
        copy.wait_send()


def shards(grid_field, row_longitudes, owner_order, legendre, vertical_band):
    lw = grid_field.shape[0]
    dma = pltpu.SemaphoreType.DMA
    vmem = pltpu.VMEM
    smem = pl.BlockSpec(memory_space=pltpu.SMEM)
    hbm = pl.BlockSpec(memory_space=pltpu.HBM)
    part_a, part_b = ZH * NI * JA, NY * NI * JB
    out = pl.pallas_call(
        kernel,
        out_shape=jax.ShapeDtypeStruct((NI, 2 * LAYERS, KW), F32),
        in_specs=[hbm, smem, smem, hbm, smem],
        out_specs=pl.BlockSpec(memory_space=pltpu.VMEM),
        scratch_shapes=[
            vmem((NN // NB, R * MW, NB), F32),
            vmem((LAYERS * R, NLON), F32),
            vmem((NA, R * LAYERS, NB), F32),
            vmem((R * 2 * KW, 3 * NB), BF16),
            vmem((R * 2 * KW, NB), F32),
            vmem((R * 2 * KW, NB), F32),
            vmem((KW // 8, NN, NB), BF16),
            vmem((NN * JA, NB), F32),
            vmem((NN * JB, NB), F32),
            vmem((NN // 2 * JA, NB), F32),
            vmem((NN // 2 * JB, NB), F32),
            vmem((2, NY // 2, 2, part_a // 2, NB), F32),
            vmem((2, ZH // 2, 2, part_b // 2, NB), F32),
            vmem(((ZH - 1) * NI * JA, NB), F32),
            vmem(((NY - 1) * NI * JB, NB), F32),
            dma((NN // NB,)), dma,
            dma((NX * ZL - 1,)), dma((NX * ZL - 1,)),
            dma((NY,)), dma((NY,)), dma((ZH,)), dma((ZH,)),
            dma((2, NY // 2, 2)), dma((2, NY // 2, 2)), dma((2, ZH // 2, 2)), dma((2, ZH // 2, 2)),
            dma((ZH - 1,)), dma((ZH - 1,)), dma((NY - 1,)), dma((NY - 1,)),
        ],
        compiler_params=pltpu.CompilerParams(
            collective_id=0, has_side_effects=True, vmem_limit_bytes=60 * 1024 * 1024
        ),
    )(
        grid_field.reshape(lw * R, NLON), row_longitudes, owner_order, legendre.reshape(R * MW, NN),
        vertical_band.transpose(1, 0, 2),
    )
    return out.reshape(NI, 2, LAYERS, KW).transpose(0, 3, 1, 2)


def solution(mesh):
    placed = (P("wave", "lat", None), P("lat"), P(), P("lat", None, None), P())
    return jax.shard_map(
        shards, mesh=mesh, in_specs=placed, out_specs=P("lat", "wave", None, None), check_vma=False
    )
```

```python
import functools

import jax
import jax.numpy as jnp
from jax import lax
from jax.experimental import pallas as pl
from jax.experimental.pallas import tpu as pltpu
from jax.sharding import PartitionSpec as P

MESH = pl.DeviceIdType.MESH
F32 = jnp.float32
BF16 = jnp.bfloat16

MW = 384
NN = 384
NLON = 768
FIELDS = 4
LEVELS = 4
LAYERS = 16
ZH = 4
NY = 8
NX = 4
ZL = 2
R = 8
KW = 48
NI = 6
NB = 128
NA = NLON // NB
JA = 8
JB = 4

COS = (1.0, -19.739208221435547, 64.93939208984375, -85.45665740966797, 60.242130279541016, -26.4046688079834,
       7.800131320953369, -1.4531123638153076)
SIN = (6.2831854820251465, -41.34170150756836, 81.6052474975586, -76.70580291748047, 42.05775451660156,
       -15.086565017700195, 3.7813189029693604, -0.6207788586616516)


def iota(shape, dim):
    return lax.broadcasted_iota(jnp.int32, shape, dim)


def split(x):
    hi = x.astype(BF16)
    return hi, (x - hi.astype(F32)).astype(BF16)


def nt(a, b):
    return lax.dot_general(a, b, (((1,), (1,)), ((), ())), preferred_element_type=F32)


def nn(a, b):
    return jnp.dot(a, b, preferred_element_type=F32)


def polynomial(coefficients, u):
    total = jnp.full_like(u, coefficients[-1])
    for c in coefficients[-2::-1]:
        total = total * u + c
    return total


def cos_sin(steps, points, inverse):
    turns = (steps - jnp.floor(steps * inverse + 0.5) * points) * inverse
    u = turns * turns
    return polynomial(COS, u), polynomial(SIN, u) * turns


def halves(extent):
    steps = []
    for s in range(extent // 2):
        for direction in (0, 1):
            for h in (0, 1):
                first = 0 if h == direction else 1
                if s >= first:
                    steps.append((direction, s, h, s > first))
    return steps


def kernel(
    grid_ref, lon_ref, order_ref, leg_ref, band_ref, out_ref,
    leg_v, gath, gx, e_s, tw_s, ft, xs, ra, rb, core_a, core_b, ring_a, far_b, half_a, half_b,
    leg_sem, own_sem, g_send, g_recv, ca_send, ca_recv, cb_send, cb_recv,
    ra_send, ra_recv, rb_send, rb_recv, da_send, da_recv, db_send, db_recv,
):
    lw = LAYERS // (NX * ZL)
    lat, wave = lax.axis_index("lat"), lax.axis_index("wave")
    core = lax.rem(lat, 2)
    y = lax.rem(lat // 2, NY)
    zh = lat // (2 * NY)
    x = wave // ZL
    zl = lax.rem(wave, ZL)

    def at_y(o, c):
        return ((zh * NY + lax.rem(y + o + NY, NY)) * 2 + c, wave)

    def at_z(o, c):
        return ((lax.rem(zh + o + ZH, ZH) * NY + y) * 2 + c, wave)

    def at_w(dx, dz):
        return (lat, lax.rem(x + dx, NX) * ZL + lax.rem(zl + dz, ZL))

    sibling = (lat + 1 - 2 * core, wave)
    wave_peers = [(dx, dz) for dx in range(NX) for dz in range(ZL) if (dx, dz) != (0, 0)]

    leg_copies = []
    for t in range(NN // NB):
        copy = pltpu.make_async_copy(leg_ref.at[:, t * NB : (t + 1) * NB], leg_v.at[t], leg_sem.at[t])
        copy.start()
        leg_copies.append(copy)
    mine = pl.ds(pl.multiple_of(wave * (lw * R), 8), lw * R)
    own_copy = pltpu.make_async_copy(grid_ref, gath.at[mine], own_sem)
    own_copy.start()

    barrier = pltpu.get_barrier_semaphore()
    both = [at_w(dx, dz) for dx, dz in wave_peers] + [sibling]

    def enter(others, expected):
        for peer in both + others:
            pl.semaphore_signal(barrier, inc=1, device_id=peer, device_id_type=MESH)
        pl.semaphore_wait(barrier, len(both) + expected)

    z_far, y_far = range(1, ZH), range(1, NY)

    @pl.when(core == 1)
    def _():
        others = [at_y(1, 1), at_y(-1, 1)] + [at_z(o, 1) for o in z_far] + [at_y(o, 0) for o in y_far]
        enter(others, 2 + 2 * (ZH - 1))

    @pl.when(core == 0)
    def _():
        others = [at_z(o, 1) for o in z_far] + [at_z(o, 0) for o in z_far] + [at_y(o, 0) for o in y_far]
        enter(others, ZH - 1 + 2 * (NY - 1))

    def remote(src, dst, send, recv, peer):
        return pltpu.make_async_remote_copy(
            src_ref=src, dst_ref=dst, send_sem=send, recv_sem=recv, device_id=peer, device_id_type=MESH
        )

    grid_copies = []
    for i, (dx, dz) in enumerate(wave_peers):
        copy = remote(grid_ref, gath.at[mine], g_send.at[i], g_recv.at[i], at_w(dx, dz))
        copy.start()
        grid_copies.append(copy)

    sub = iota((8, NB), 0)
    waves = []
    for t in range(KW // 8):
        column = jnp.zeros((8, NB), F32)
        for s in range(8):
            column = jnp.where(sub == s, order_ref[wave * KW + t * 8 + s].astype(F32), column)
        waves.append(column)
    waves = jnp.concatenate(waves, axis=0)

    lane = iota((KW, NB), 1)
    low = lane.astype(F32)
    high = ((lane // LAYERS) * NB).astype(F32)
    for r in range(R):
        points = jnp.full((KW, NB), lon_ref[r], jnp.int32).astype(F32)
        inverse = 1.0 / points
        cos_low, sin_low = cos_sin(waves * low, points, inverse)
        table_hi, table_lo = split(jnp.concatenate([cos_low, -sin_low], axis=0))
        e_s[r * 2 * KW : (r + 1) * 2 * KW, :] = jnp.concatenate([table_hi, table_hi, table_lo], axis=1)
        cos_high, sin_high = cos_sin(waves * high, points, inverse)
        factor = jnp.where(2.0 * waves < points, 1.0 / jnp.sqrt(points), 0.0)
        tw_s[r * 2 * KW : r * 2 * KW + KW, :] = cos_high * factor
        tw_s[r * 2 * KW + KW : (r + 1) * 2 * KW, :] = -sin_high * factor

    n_lane = iota((1, NN), 1).astype(F32) + 0.5
    z_of = jnp.floor(n_lane * (1.0 / (NI * 2 * NY)))
    rest = n_lane - z_of * (NI * 2 * NY)
    y_of = jnp.floor(rest * (1.0 / (NI * 2)))
    rest = rest - y_of * (NI * 2)
    c_of = jnp.floor(rest * (1.0 / NI))
    i_of = rest - c_of * NI - 0.5
    z_rel = z_of - zh.astype(F32)
    z_rel = jnp.where(z_rel < 0, z_rel + ZH, z_rel)
    y_rel = y_of - y.astype(F32)
    y_rel = jnp.where(y_rel < 0, y_rel + NY, y_rel)
    n_row = iota((NN, NN), 0).astype(F32)
    place_a = ((y_rel * ZH + z_rel) * 2 + c_of) * NI + i_of
    place_b = ((z_rel * NY + y_rel) * 2 + c_of) * NI + i_of
    order_a = jnp.where(n_row == place_a, 1.0, 0.0).astype(BF16)
    order_b = jnp.where(n_row == place_b, 1.0, 0.0).astype(BF16)

    def slot(g, q):
        return (q % 4) * (KW // 4) + 2 * g + q // 4

    groups = KW // 8
    for copy in leg_copies:
        copy.wait()
    n_of = iota((R, NN), 1)
    for g in range(groups):
        rows = []
        for q in range(8):
            m = order_ref[wave * KW + slot(g, q)]
            picked = jnp.concatenate([leg_v[t, pl.ds(m, R, stride=MW), :] for t in range(NN // NB)], axis=1)
            rows.append(jnp.where(n_of >= m, picked, 0.0))
        hi, lo = split(jnp.concatenate(rows, axis=0))
        turned = nt(order_a if 2 * g < JA else order_b, jnp.concatenate([hi, lo], axis=0))
        xs[g] = turned.astype(BF16)

    own_copy.wait()
    for copy in grid_copies:
        copy.wait_recv()
    for layer in range(LAYERS):
        for a in range(NA):
            gx[a, pl.ds(layer, R, stride=LAYERS), :] = gath[layer * R : (layer + 1) * R, a * NB : (a + 1) * NB]

    spread = jnp.where(iota((2 * NB, NB), 0) % LAYERS == iota((2 * NB, NB), 1) % LAYERS, 1.0, 0.0).astype(BF16)
    column = iota((LAYERS, NB), 1)
    for r in range(R):
        points = lon_ref[r]
        parts = [
            jnp.where(column + a * NB < points, gx[a, r * LAYERS : (r + 1) * LAYERS, :], 0.0) for a in range(NA)
        ]
        parts += [jnp.zeros((LAYERS, NB), F32)] * (NB // LAYERS - NA)
        hi, lo = split(jnp.concatenate(parts, axis=0))
        first = nt(e_s[r * 2 * KW : (r + 1) * 2 * KW, :], jnp.concatenate([hi, lo, hi], axis=1))
        re, im = first[:KW], first[KW:]
        tw_re = tw_s[r * 2 * KW : r * 2 * KW + KW, :]
        tw_im = tw_s[r * 2 * KW + KW : (r + 1) * 2 * KW, :]
        both = jnp.concatenate([re * tw_re - im * tw_im, re * tw_im + im * tw_re], axis=0)
        hi, lo = split(both)
        ft[r * 2 * KW : (r + 1) * 2 * KW, :] = nn(jnp.concatenate([hi, lo], axis=1), spread)

    lanes = iota((R, NB), 1)
    k4_of = lanes // (2 * LAYERS)
    is_cos = (lanes // LAYERS) % 2 == 0
    diagonals = []
    for g in range(groups):
        rows = []
        for q in range(8):
            k = slot(g, q)
            value = jnp.where(is_cos, ft[pl.ds(k, R, stride=2 * KW), :], ft[pl.ds(KW + k, R, stride=2 * KW), :])
            value = jnp.where(k4_of == q % 4, value, 0.0)
            zero = jnp.zeros((R, NB), F32)
            rows.append(jnp.concatenate([value, zero] if q < 4 else [zero, value], axis=1))
        hi, lo = split(jnp.concatenate(rows, axis=0))
        diagonals.append(jnp.concatenate([hi, hi, lo, lo], axis=0))

    def partial_sums(first, last):
        for g in range(first, last):
            turned = xs[g]
            sums = nn(jnp.concatenate([turned, turned], axis=1), diagonals[g])
            for t in (0, 1):
                j = 2 * g + t
                value = sums[:, t * NB : (t + 1) * NB]
                if j < JA:
                    ra[pl.ds(j, NN, stride=JA), :] = value
                else:
                    rb[pl.ds(j - JA, NN, stride=JB), :] = value

    part_a = NN // NY * JA
    part_b = NN // ZH * JB
    rows_a, rows_b = NI * JA, NI * JB
    y_order = sorted(range(NY), key=lambda o: -min(o, NY - o))
    z_order = sorted(range(ZH), key=lambda o: -min(o, ZH - o))
    cut = JA // 2

    def core_a_copy(o):
        rows = pl.ds(o * part_a, part_a)
        return remote(ra.at[rows], core_a.at[rows], ca_send.at[o], ca_recv.at[o], sibling)

    def core_b_copy(o):
        rows = pl.ds(o * part_b, part_b)
        return remote(rb.at[rows], core_b.at[rows], cb_send.at[o], cb_recv.at[o], sibling)

    def ring_copy(direction, s, h):
        o = NY // 2 - s if direction == 0 else NY // 2 + s
        rows = pl.ds(o * part_a + h * (part_a // 2), part_a // 2)
        return remote(
            ra.at[rows], ring_a.at[direction, s, h], ra_send.at[direction, s, h], ra_recv.at[direction, s, h],
            at_y(1 if direction == 0 else -1, 1),
        )

    def far_copy(o):
        return remote(
            rb.at[pl.ds(o * part_b, part_b)], far_b.at[pl.ds((o - 1) * part_b, part_b)],
            rb_send.at[o - 1], rb_recv.at[o - 1], at_z(o, 0),
        )

    def end_a_copy(o, c):
        return remote(
            ra.at[pl.ds((o * 2 + c) * rows_a, rows_a)], half_a.at[pl.ds(o * rows_a, rows_a)],
            da_send.at[o, c], da_recv.at[o], at_z(o, c) if o else sibling,
        )

    def end_b_copy(o, c):
        return remote(
            rb.at[pl.ds((o * 2 + c) * rows_b, rows_b)], half_b.at[pl.ds(o * rows_b, rows_b)],
            db_send.at[o, c], db_recv.at[o], at_y(o, c) if o else sibling,
        )

    end_a = [(o, c) for o in z_order for c in (0, 1) if (o, c) != (0, 1)]
    end_b = [(o, c) for o in y_order for c in (0, 1) if (o, c) != (0, 0)]

    @pl.when(core == 1)
    def _():
        partial_sums(cut, groups)
        for o in z_order:
            core_b_copy(o).start()
        partial_sums(0, cut)
        seen = set()

        def own_part(o):
            if o not in seen:
                seen.add(o)
                core_a_copy(o).wait_recv()
                rows = pl.ds(o * part_a, part_a)
                ra[rows, :] = ra[rows, :] + core_a[rows, :]

        for direction, s, h, has in halves(NY):
            o = NY // 2 - s if direction == 0 else NY // 2 + s
            own_part(o)
            if has:
                rows = pl.ds(o * part_a + h * (part_a // 2), part_a // 2)
                ring_copy(direction, s - 1, h).wait_recv()
                ra[rows, :] = ra[rows, :] + ring_a[direction, s - 1, h]
            ring_copy(direction, s, h).start()
        own_part(0)
        last = NY // 2 - 1
        for h in (0, 1):
            rows = pl.ds(h * (part_a // 2), part_a // 2)
            total = ra[rows, :]
            for direction in (0, 1):
                if (direction, last, h) in [item[:3] for item in halves(NY)]:
                    ring_copy(direction, last, h).wait_recv()
                    total = total + ring_a[direction, last, h]
            ra[rows, :] = total
        for o, c in end_a:
            end_a_copy(o, c).start()
        half_a[:rows_a, :] = ra[rows_a : 2 * rows_a, :]
        end_b_copy(0, 1).wait_recv()

    @pl.when(core == 0)
    def _():
        partial_sums(0, cut)
        for o in y_order:
            core_a_copy(o).start()
        partial_sums(cut, groups)
        for o in z_order:
            core_b_copy(o).wait_recv()
            rows = pl.ds(o * part_b, part_b)
            rb[rows, :] = rb[rows, :] + core_b[rows, :]
            if o:
                far_copy(o).start()
        total = rb[:part_b, :]
        for o in z_far:
            far_copy(o).wait_recv()
            total = total + far_b[(o - 1) * part_b : o * part_b, :]
        rb[:part_b, :] = total
        for o, c in end_b:
            end_b_copy(o, c).start()
        half_b[:rows_b, :] = rb[:rows_b, :]
        end_a_copy(0, 0).wait_recv()

    band = [jnp.zeros((1, NB), F32) for _ in range(3)]
    layer_of = iota((1, NB), 1) % LAYERS
    for d in range(3):
        for f in range(FIELDS):
            for l in range(LEVELS):
                if (d, l) in ((0, 0), (2, LEVELS - 1)):
                    continue
                band[d] = jnp.where(layer_of == f * LEVELS + l, band_ref[d, f, l], band[d])

    def vertical(total, width):
        degree = iota(total.shape, 0) // width + lat * NI
        degree = degree.astype(F32)
        ratio = degree * (degree + 1.0) * (1.0 / (MW * MW))
        below = pltpu.roll(total, 1, 1)
        above = pltpu.roll(total, NB - 1, 1)
        return total + ratio * (band[0] * below + band[1] * total + band[2] * above)

    total_b = half_b[:rows_b, :]
    for o in y_far:
        end_b_copy(o, 0).wait_recv()
        total_b = total_b + half_b[o * rows_b : (o + 1) * rows_b, :]
    total_b = vertical(total_b, JB)
    total_a = half_a[:rows_a, :]
    for o in z_far:
        end_a_copy(o, 0).wait_recv()
        total_a = total_a + half_a[o * rows_a : (o + 1) * rows_a, :]
    total_a = vertical(total_a, JA)

    fill = jnp.zeros((NB - rows_a - rows_b, NB), F32)
    turned = jnp.concatenate([total_a, total_b, fill], axis=0).T
    cl = 2 * LAYERS
    for i in range(NI):
        pieces = []
        for k4 in range(4):
            rows = turned[k4 * cl : (k4 + 1) * cl]
            pieces.append(rows[:, i * JA : (i + 1) * JA])
            pieces.append(rows[:, rows_a + i * JB : rows_a + (i + 1) * JB])
        out_ref[i] = jnp.concatenate(pieces, axis=1)

    for copy in grid_copies:
        copy.wait_send()

    @pl.when(core == 1)
    def _():
        for o in z_order:
            core_b_copy(o).wait_send()
        for direction, s, h, _ in halves(NY):
            ring_copy(direction, s, h).wait_send()
        for o, c in end_a:
            end_a_copy(o, c).wait_send()

    @pl.when(core == 0)
    def _():
        for o in y_order:
            core_a_copy(o).wait_send()
        for o in z_far:
            far_copy(o).wait_send()
        for o, c in end_b:
            end_b_copy(o, c).wait_send()


def shards(grid_field, row_longitudes, owner_order, legendre, vertical_band):
    lw = grid_field.shape[0]
    dma = pltpu.SemaphoreType.DMA
    vmem = pltpu.VMEM
    smem = pl.BlockSpec(memory_space=pltpu.SMEM)
    hbm = pl.BlockSpec(memory_space=pltpu.HBM)
    part_a, part_b = NN // NY * JA, NN // ZH * JB
    out = pl.pallas_call(
        kernel,
        out_shape=jax.ShapeDtypeStruct((NI, 2 * LAYERS, KW), F32),
        in_specs=[hbm, smem, smem, hbm, smem],
        out_specs=pl.BlockSpec(memory_space=pltpu.VMEM),
        scratch_shapes=[
            vmem((NN // NB, R * MW, NB), F32),
            vmem((LAYERS * R, NLON), F32),
            vmem((NA, R * LAYERS, NB), F32),
            vmem((R * 2 * KW, 3 * NB), BF16),
            vmem((R * 2 * KW, NB), F32),
            vmem((R * 2 * KW, NB), F32),
            vmem((KW // 8, NN, NB), BF16),
            vmem((NN * JA, NB), F32),
            vmem((NN * JB, NB), F32),
            vmem((NN * JA, NB), F32),
            vmem((NN * JB, NB), F32),
            vmem((2, NY // 2, 2, part_a // 2, NB), F32),
            vmem(((ZH - 1) * part_b, NB), F32),
            vmem((ZH * NI * JA, NB), F32),
            vmem((NY * NI * JB, NB), F32),
            dma((NN // NB,)), dma,
            dma((NX * ZL - 1,)), dma((NX * ZL - 1,)),
            dma((NY,)), dma((NY,)), dma((ZH,)), dma((ZH,)),
            dma((2, NY // 2, 2)), dma((2, NY // 2, 2)), dma((ZH - 1,)), dma((ZH - 1,)),
            dma((ZH, 2)), dma((ZH,)), dma((NY, 2)), dma((NY,)),
        ],
        compiler_params=pltpu.CompilerParams(
            collective_id=0, has_side_effects=True, vmem_limit_bytes=60 * 1024 * 1024
        ),
    )(
        grid_field.reshape(lw * R, NLON), row_longitudes, owner_order, legendre.reshape(R * MW, NN),
        vertical_band.transpose(1, 0, 2),
    )
    return out.reshape(NI, 2, LAYERS, KW).transpose(0, 3, 1, 2)


def solution(mesh):
    placed = (P("wave", "lat", None), P("lat"), P(), P("lat", None, None), P())
    return jax.shard_map(
        shards, mesh=mesh, in_specs=placed, out_specs=P("lat", "wave", None, None), check_vma=False
    )
```

```python
import functools

import jax
import jax.numpy as jnp
from jax import lax
from jax.experimental import pallas as pl
from jax.experimental.pallas import tpu as pltpu
from jax.sharding import PartitionSpec as P

MESH = pl.DeviceIdType.MESH
F32 = jnp.float32
BF16 = jnp.bfloat16

MW = 384
NN = 384
NLON = 768
FIELDS = 4
LEVELS = 4
LAYERS = 16
ZH = 4
NY = 8
NX = 4
ZL = 2
R = 8
KW = 48
NI = 6
NB = 128
NA = NLON // NB
JA = 8
JB = 4

QUARTER_SIN = (6.2831854820251465, -41.34168243408203, 81.60247802734375, -76.58128356933594, 39.76072311401367)
QUARTER_COS = (0.9999999403953552, -19.739171981811523, 64.93457794189453, -85.24009704589844, 56.24053955078125)
COS = (1.0, -19.739208221435547, 64.93939208984375, -85.45665740966797, 60.242130279541016, -26.4046688079834,
       7.800131320953369, -1.4531123638153076)
SIN = (6.2831854820251465, -41.34170150756836, 81.6052474975586, -76.70580291748047, 42.05775451660156,
       -15.086565017700195, 3.7813189029693604, -0.6207788586616516)


def iota(shape, dim):
    return lax.broadcasted_iota(jnp.int32, shape, dim)


def split(x):
    hi = x.astype(BF16)
    return hi, (x - hi.astype(F32)).astype(BF16)


def nt(a, b):
    return lax.dot_general(a, b, (((1,), (1,)), ((), ())), preferred_element_type=F32)


def nn(a, b):
    return jnp.dot(a, b, preferred_element_type=F32)


def polynomial(coefficients, u):
    total = jnp.full_like(u, coefficients[-1])
    for c in coefficients[-2::-1]:
        total = total * u + c
    return total


def cos_sin(steps, points, inverse):
    turns = (steps - jnp.floor(steps * inverse + 0.5) * points) * inverse
    u = turns * turns
    return polynomial(COS, u), polynomial(SIN, u) * turns


PIECES = 4


def ring_pieces(extent):
    return [
        (direction, s, q)
        for s in range(extent // 2)
        for late in (0, 1)
        for q in range(PIECES)
        for direction in (0, 1)
        if late == (1 if (q < PIECES // 2) == (direction == 1) else 0) and s >= late
    ]


def chunk_of(extent, direction, s):
    return extent // 2 - s if direction == 0 else extent // 2 + s


def kernel(
    grid_ref, lon_ref, order_ref, leg_ref, band_ref, out_ref,
    leg_v, gv, xr, e_s, x_s, packets, arrived, picked_out, picked_in, xs, ra, rb, ring_a, ring_b, half_a, half_b,
    leg_sem, own_sem, leg_send, leg_recv, g_send, g_recv,
    ra_send, ra_recv, rb_send, rb_recv, da_send, da_recv, db_send, db_recv,
):
    lat, wave = lax.axis_index("lat"), lax.axis_index("wave")
    core = lax.rem(lat, 2)
    y = lax.rem(lat // 2, NY)
    zh = lat // (2 * NY)
    x = wave // ZL
    zl = lax.rem(wave, ZL)

    def at_y(o, c):
        return ((zh * NY + lax.rem(y + o + NY, NY)) * 2 + c, wave)

    def at_z(o, c):
        return ((lax.rem(zh + o + ZH, ZH) * NY + y) * 2 + c, wave)

    def wave_at(dx, dz):
        return lax.rem(x + dx, NX) * ZL + lax.rem(zl + dz, ZL)

    def at_w(dx, dz, dc):
        return (lat - core + lax.rem(core + dc, 2), wave_at(dx, dz))

    sibling = (lat + 1 - 2 * core, wave)
    wave_peers = [(dx, dz, dc) for dx in range(NX) for dz in range(ZL) for dc in (0, 1)][1:]
    wave_peers.sort(key=lambda to: -min(to[0], NX - to[0]) - to[1])

    leg_copies = []
    for t in range(NN // NB):
        copy = pltpu.make_async_copy(leg_ref.at[:, t * NB : (t + 1) * NB], leg_v.at[t], leg_sem.at[t])
        copy.start()
        leg_copies.append(copy)
    own_copy = pltpu.make_async_copy(grid_ref, gv, own_sem)
    own_copy.start()

    barrier = pltpu.get_barrier_semaphore()
    both = [at_w(*to) for to in wave_peers]

    def enter(others):
        for peer in both + others:
            pl.semaphore_signal(barrier, inc=1, device_id=peer, device_id_type=MESH)

    z_far, y_far = range(1, ZH), range(1, NY)

    @pl.when(core == 1)
    def _():
        others = [at_y(1, 1), at_y(-1, 1)] + [at_z(o, 1) for o in z_far] + [at_y(o, 0) for o in y_far]
        enter(others)

    @pl.when(core == 0)
    def _():
        others = [at_z(o, 1) for o in z_far] + [at_z(o, 0) for o in z_far] + [at_y(o, 0) for o in y_far]
        enter(others)

    def remote(src, dst, send, recv, peer):
        return pltpu.make_async_remote_copy(
            src_ref=src, dst_ref=dst, send_sem=send, recv_sem=recv, device_id=peer, device_id_type=MESH
        )

    sub = iota((8, NB), 0)
    rows_of = [
        (g * KW + k4 * (KW // 4), p) for g in range(8) for p in range(JA) for k4 in range(4)
    ] + [(g * KW + k4 * (KW // 4) + JA, p + JA) for g in range(8) for p in range(JB) for k4 in range(4)]
    turn_a = [lax.rem(p + JA - wave, JA) for p in range(JA)]
    turn_b = [lax.rem(p + 2 * JB - wave, JB) for p in range(JB)]
    shift = turn_a + turn_b
    waves = []
    for t in range(len(rows_of) // 8):
        column = jnp.zeros((8, NB), F32)
        for i in range(8):
            base, p = rows_of[t * 8 + i]
            column = jnp.where(sub == i, order_ref[base + shift[p]].astype(F32), column)
        waves.append(column)
    waves = jnp.concatenate(waves, axis=0)
    slots = len(rows_of)

    own_copy.wait()
    sub = iota((2 * R, NB), 0)
    points = jnp.zeros((2 * R, NB), jnp.int32)
    for r in range(R):
        points = jnp.where(sub % R == r, lon_ref[r], points)
    column = iota((2 * R, NB), 1)
    for a in range(8):
        if a < NA:
            value = jnp.where(column + a * NB < points, gv[:, a * NB : (a + 1) * NB], 0.0)
        else:
            value = jnp.zeros((2 * R, NB), F32)
        xr[pl.ds(a, 2 * R, stride=8), :] = value

    low = iota((1, NB), 1).astype(F32)
    row_of = (iota((NB, NB), 0) // 8) % R
    for r in range(R):
        inverse = 1.0 / jnp.full((1, NB), lon_ref[r], jnp.int32).astype(F32)
        u = waves * (low * inverse)
        u = u - jnp.floor(u + 0.5)
        v = jnp.abs(u) - 0.25
        square = v * v
        cosine = -v * polynomial(QUARTER_SIN, square)
        sine = polynomial(QUARTER_COS, square)
        minus_sine = jnp.where(u < 0, sine, -sine)
        for c, table in enumerate((cosine, minus_sine)):
            hi, lo = split(table)
            e_s[c * slots : (c + 1) * slots, r * 2 * NB : (r * 2 + 1) * NB] = hi
            e_s[c * slots : (c + 1) * slots, (r * 2 + 1) * NB : (r * 2 + 2) * NB] = lo
        hi, lo = split(jnp.where(row_of == r, xr[...], 0.0))
        for t in (0, 1):
            x_s[:NB, (r * 2 + t) * NB : (r * 2 + t + 1) * NB] = hi
            x_s[NB:, (r * 2 + t) * NB : (r * 2 + t + 1) * NB] = lo
    first = nt(e_s[...], x_s[...])
    first = first[:, :NB] + first[:, NB:]

    lane = iota((1, NB), 1)
    points = jnp.zeros((1, NB), jnp.int32)
    for r in range(R):
        points = jnp.where((lane // 8) % R == r, lon_ref[r], points)
    points = points.astype(F32)
    high = ((lane % 8) * NB).astype(F32)
    tw_re, tw_im = cos_sin(waves * high, points, 1.0 / points)
    factor = jnp.where(2.0 * waves < points, 1.0 / jnp.sqrt(points), 0.0)
    tw_re, tw_im = tw_re * factor, -tw_im * factor
    re, im = first[:slots], first[slots:]
    both_parts = jnp.concatenate([re * tw_re - im * tw_im, re * tw_im + im * tw_re], axis=0)
    hi, lo = split(both_parts)
    gather = jnp.where(iota((2 * R, NB), 1) // 8 == iota((2 * R, NB), 0), 1.0, 0.0).astype(BF16)
    spectrum = nt(jnp.concatenate([gather, gather], axis=1), jnp.concatenate([hi, lo], axis=1))

    part_of_a = JA * 4
    for g in range(8):
        for c_to in (0, 1):
            blocks = []
            for layer in (0, 1):
                for c in (0, 1):
                    value = spectrum[layer * R : (layer + 1) * R, c * slots : (c + 1) * slots]
                    if c_to == 1:
                        blocks.append(value[:, g * part_of_a : (g + 1) * part_of_a])
                    else:
                        start = 8 * part_of_a + g * JB * 4
                        blocks += [value[:, start : start + JB * 4]] * 2
            packets[c_to, g] = jnp.concatenate(blocks, axis=1)

    @pl.when(core == 1)
    def _():
        pl.semaphore_wait(barrier, len(both) + 2 + 2 * (ZH - 1))

    @pl.when(core == 0)
    def _():
        pl.semaphore_wait(barrier, len(both) + ZH - 1 + 2 * (NY - 1))

    def packet_copy(i):
        dx, dz, dc = wave_peers[i]
        return remote(
            packets.at[lax.rem(core + dc, 2), wave_at(dx, dz)], arrived.at[core, wave],
            g_send.at[i], g_recv.at[i], at_w(dx, dz, dc),
        )

    for i in range(len(wave_peers)):
        packet_copy(i).start()
    arrived[core, wave] = packets[core, wave]

    n_lane = iota((1, NN), 1).astype(F32) + 0.5
    z_of = jnp.floor(n_lane * (1.0 / (NI * 2 * NY)))
    rest = n_lane - z_of * (NI * 2 * NY)
    y_of = jnp.floor(rest * (1.0 / (NI * 2)))
    rest = rest - y_of * (NI * 2)
    c_of = jnp.floor(rest * (1.0 / NI))
    i_of = rest - c_of * NI - 0.5
    z_rel = z_of - zh.astype(F32)
    z_rel = jnp.where(z_rel < 0, z_rel + ZH, z_rel)
    y_rel = y_of - y.astype(F32)
    y_rel = jnp.where(y_rel < 0, y_rel + NY, y_rel)
    place_a = ((y_rel * ZH + z_rel) * 2 + c_of) * NI + i_of
    place_b = ((z_rel * NY + y_rel) * 2 + c_of) * NI + i_of
    place = jnp.where(core == 1, place_a, place_b)

    def slot(g, q):
        return (q % 4) * (KW // 4) + 2 * g + q // 4

    groups = KW // 8
    cut = JA // 2
    near, far = cut * 8, (groups - cut) * 8
    for copy in leg_copies:
        copy.wait()
    n_of = iota((R, NN), 1)

    def pick(g, q):
        m = order_ref[wave * KW + slot(g, q)]
        picked = jnp.concatenate([leg_v[t, pl.ds(m, R, stride=MW), :] for t in range(NN // NB)], axis=1)
        return jnp.where(n_of >= m, picked, 0.0)

    def rows_copy(c_from):
        count = far if c_from == 1 else near
        return remote(
            picked_out.at[pl.ds(0, count)], picked_in.at[pl.ds(0, count), c_from], leg_send, leg_recv, sibling
        )

    @pl.when(core == 1)
    def _():
        for at in range(far):
            picked_out[at] = pick(cut + at // 8, at % 8)
        rows_copy(1).start()
        for at in range(near):
            picked_in[at, 1] = pick(at // 8, at % 8)

    @pl.when(core == 0)
    def _():
        for at in range(near):
            picked_out[at] = pick(at // 8, at % 8)
        rows_copy(0).start()
        for at in range(far):
            picked_in[at, 0] = pick(cut + at // 8, at % 8)

    order = jnp.where(iota((NN, NN), 0).astype(F32) == place, 1.0, 0.0).astype(BF16)

    def turn_rows(count):
        for g in range(count // 8):
            hi, lo = split(picked_in[g * 8 : (g + 1) * 8].reshape(8 * 2 * R, NN))
            xs[g] = nt(order, jnp.concatenate([hi, lo], axis=0)).astype(BF16)

    lanes = iota((2 * R, NB), 1)
    k4_of = lanes % 4
    place_of = (lanes // 4) % 8
    per_core = 2 * R

    def values_of(j):
        total = jnp.zeros((per_core, NB), F32)
        for g in range(8):
            value = jnp.concatenate([arrived[0, g], arrived[1, g]], axis=0)
            total = jnp.where(place_of == (j + g) % 8, value, total)
        if j == 0:
            return total
        near_roll = pltpu.roll(total, NB - 4 * j, 1)
        far_roll = pltpu.roll(total, 32 - 4 * j, 1)
        return jnp.where(place_of + j < 8, near_roll, far_roll)

    def partial_sums(count, target, width):
        for g in range(count):
            rows = []
            zero = jnp.zeros((per_core, NB), F32)
            for t in (0, 1):
                value = values_of(2 * g + t)
                for k4 in range(4):
                    one = jnp.where(k4_of == k4, value, 0.0)
                    rows.append(jnp.concatenate([zero, one] if t else [one, zero], axis=1))
            hi, lo = split(jnp.concatenate(rows, axis=0))
            turned = xs[g]
            sums = nn(turned, jnp.concatenate([hi, hi], axis=0)) + nn(turned[:, :NB], lo)
            for t in (0, 1):
                target[pl.ds(2 * g + t, NN, stride=width), :] = sums[:, t * NB : (t + 1) * NB]

    part_a = NN // NY * JA
    part_b = NN // ZH * JB
    rows_a, rows_b = NI * JA, NI * JB
    y_order = sorted(range(NY), key=lambda o: -min(o, NY - o))
    z_order = sorted(range(ZH), key=lambda o: -min(o, ZH - o))
    def piece_rows(part, o, q):
        return pl.ds(o * part + q * (part // PIECES), part // PIECES)

    def ring_a_copy(direction, s, q):
        return remote(
            ra.at[piece_rows(part_a, chunk_of(NY, direction, s), q)], ring_a.at[direction, s, q],
            ra_send.at[direction, s, q], ra_recv.at[direction, s, q], at_y(1 - 2 * direction, 1),
        )

    def ring_b_copy(direction, s, q):
        return remote(
            rb.at[piece_rows(part_b, chunk_of(ZH, direction, s), q)], ring_b.at[direction, s, q],
            rb_send.at[direction, s, q], rb_recv.at[direction, s, q], at_z(1 - 2 * direction, 0),
        )

    def reduce_ring(extent, part, own, landing, copy, finish):
        every = ring_pieces(extent)

        first = [p for p in every if (p[0], p[1] - 1, p[2]) not in every]
        for p in first + [p for p in every if p not in first]:
            direction, s, q = p
            o = chunk_of(extent, direction, s)
            if p not in first:
                rows = piece_rows(part, o, q)
                copy(direction, s - 1, q).wait_recv()
                own[rows, :] = own[rows, :] + landing[direction, s - 1, q]
            copy(*p).start()
        last = extent // 2 - 1
        for q in range(PIECES):
            rows = piece_rows(part, 0, q)
            total = own[rows, :]
            for direction in (0, 1):
                if (direction, last, q) in every:
                    copy(direction, last, q).wait_recv()
                    total = total + landing[direction, last, q]
            own[rows, :] = total
            finish(q)

    def end_a_copy(o, c):
        return remote(
            ra.at[pl.ds((o * 2 + c) * rows_a, rows_a)], half_a.at[pl.ds(o * rows_a, rows_a)],
            da_send.at[o, c], da_recv.at[o], at_z(o, c) if o else sibling,
        )

    def end_b_copy(o, c):
        return remote(
            rb.at[pl.ds((o * 2 + c) * rows_b, rows_b)], half_b.at[pl.ds(o * rows_b, rows_b)],
            db_send.at[o, c], db_recv.at[o], at_y(o, c) if o else sibling,
        )

    end_a = [(o, c) for o in z_order for c in (0, 1) if (o, c) != (0, 1)]
    end_b = [(o, c) for o in y_order for c in (0, 1) if (o, c) != (0, 0)]

    @pl.when(core == 1)
    def _():
        rows_copy(0).wait_recv()
        turn_rows(near)
        for i in range(len(wave_peers)):
            packet_copy(i).wait_recv()
        partial_sums(cut, ra, JA)

        def finish(q):
            for o, c in end_a:
                if (o * 2 + c) * rows_a // (part_a // PIECES) == q:
                    end_a_copy(o, c).start()

        reduce_ring(NY, part_a, ra, ring_a, ring_a_copy, finish)
        half_a[:rows_a, :] = ra[rows_a : 2 * rows_a, :]
        end_b_copy(0, 1).wait_recv()

    @pl.when(core == 0)
    def _():
        rows_copy(1).wait_recv()
        turn_rows(far)
        for i in range(len(wave_peers)):
            packet_copy(i).wait_recv()
        partial_sums(groups - cut, rb, JB)

        def finish(q):
            for o, c in end_b:
                if (o * 2 + c) * rows_b // (part_b // PIECES) == q:
                    end_b_copy(o, c).start()

        reduce_ring(ZH, part_b, rb, ring_b, ring_b_copy, finish)
        half_b[:rows_b, :] = rb[:rows_b, :]
        end_a_copy(0, 0).wait_recv()

    band = [jnp.zeros((1, NB), F32) for _ in range(3)]
    lane = iota((1, NB), 1)
    odd = lane // (NB // 2)
    layer_of = 2 * ((lane // 4) % 8) + odd
    for d in range(3):
        for f in range(FIELDS):
            for l in range(LEVELS):
                if (d, l) in ((0, 0), (2, LEVELS - 1)):
                    continue
                band[d] = jnp.where(layer_of == f * LEVELS + l, band_ref[d, f, l], band[d])

    def vertical(total, width):
        degree = iota(total.shape, 0) // width + lat * NI
        degree = degree.astype(F32)
        ratio = degree * (degree + 1.0) * (1.0 / (MW * MW))
        other = pltpu.roll(total, NB // 2, 1)
        below = jnp.where(odd == 1, other, pltpu.roll(total, NB // 2 + 4, 1))
        above = jnp.where(odd == 0, other, pltpu.roll(total, NB // 2 - 4, 1))
        return total + ratio * (band[0] * below + band[1] * total + band[2] * above)

    total_b = half_b[:rows_b, :]
    for o in y_far:
        end_b_copy(o, 0).wait_recv()
        total_b = total_b + half_b[o * rows_b : (o + 1) * rows_b, :]
    total_b = vertical(total_b, JB)
    total_a = half_a[:rows_a, :]
    for o in z_far:
        end_a_copy(o, 0).wait_recv()
        total_a = total_a + half_a[o * rows_a : (o + 1) * rows_a, :]
    total_a = vertical(total_a, JA)

    total = jnp.concatenate([total_a, total_b], axis=0)
    hi, lo = split(total)
    rest = (total - hi.astype(F32) - lo.astype(F32)).astype(BF16)
    row, lane = iota((NB, NB), 0), iota((NB, NB), 1)
    cl = 2 * LAYERS
    source = (row % 2) * 64 + ((row % cl) // LAYERS) * 32 + ((row % LAYERS) // 2) * 4 + row // cl
    chosen = jnp.where(lane == source, 1.0, 0.0).astype(BF16)
    turned = nt(jnp.concatenate([chosen] * 3, axis=1), jnp.concatenate([hi, lo, rest], axis=1))
    for i in range(NI):
        pieces = []
        for k4 in range(4):
            rows = turned[k4 * cl : (k4 + 1) * cl]
            pieces.append(rows[:, i * JA : (i + 1) * JA])
            pieces.append(rows[:, rows_a + i * JB : rows_a + (i + 1) * JB])
        out_ref[i] = jnp.concatenate(pieces, axis=1)

    for i in range(len(wave_peers)):
        packet_copy(i).wait_send()

    @pl.when(core == 1)
    def _():
        rows_copy(1).wait_send()
        for p in ring_pieces(NY):
            ring_a_copy(*p).wait_send()
        for o, c in end_a:
            end_a_copy(o, c).wait_send()

    @pl.when(core == 0)
    def _():
        rows_copy(0).wait_send()
        for p in ring_pieces(ZH):
            ring_b_copy(*p).wait_send()
        for o, c in end_b:
            end_b_copy(o, c).wait_send()


def shards(grid_field, row_longitudes, owner_order, legendre, vertical_band):
    lw = grid_field.shape[0]
    dma = pltpu.SemaphoreType.DMA
    vmem = pltpu.VMEM
    smem = pl.BlockSpec(memory_space=pltpu.SMEM)
    hbm = pl.BlockSpec(memory_space=pltpu.HBM)
    part_a, part_b = NN // NY * JA, NN // ZH * JB
    out = pl.pallas_call(
        kernel,
        out_shape=jax.ShapeDtypeStruct((NI, 2 * LAYERS, KW), F32),
        in_specs=[hbm, smem, smem, hbm, smem],
        out_specs=pl.BlockSpec(memory_space=pltpu.VMEM),
        scratch_shapes=[
            vmem((NN // NB, R * MW, NB), F32),
            vmem((2 * R, NLON), F32),
            vmem((NB, NB), F32),
            vmem((2 * MW, R * 2 * NB), BF16),
            vmem((2 * NB, R * 2 * NB), BF16),
            vmem((2, 8, R, NB), F32),
            vmem((2, 8, R, NB), F32),
            vmem((JA * 4, R, NN), F32),
            vmem((JA * 4, 2, R, NN), F32),
            vmem((JA // 2, NN, 2 * NB), BF16),
            vmem((NN * JA, NB), F32),
            vmem((NN * JB, NB), F32),
            vmem((2, NY // 2, PIECES, part_a // PIECES, NB), F32),
            vmem((2, ZH // 2, PIECES, part_b // PIECES, NB), F32),
            vmem((ZH * NI * JA, NB), F32),
            vmem((NY * NI * JB, NB), F32),
            dma((NN // NB,)), dma, dma, dma,
            dma((2 * NX * ZL - 1,)), dma((2 * NX * ZL - 1,)),
            dma((2, NY // 2, PIECES)), dma((2, NY // 2, PIECES)),
            dma((2, ZH // 2, PIECES)), dma((2, ZH // 2, PIECES)),
            dma((ZH, 2)), dma((ZH,)), dma((NY, 2)), dma((NY,)),
        ],
        compiler_params=pltpu.CompilerParams(
            collective_id=0, has_side_effects=True, vmem_limit_bytes=60 * 1024 * 1024
        ),
    )(
        grid_field.reshape(lw * R, NLON), row_longitudes, owner_order, legendre.reshape(R * MW, NN),
        vertical_band.transpose(1, 0, 2),
    )
    return out.reshape(NI, 2, LAYERS, KW).transpose(0, 3, 1, 2)


def solution(mesh):
    placed = (P("wave", "lat", None), P("lat"), P(), P("lat", None, None), P())
    return jax.shard_map(
        shards, mesh=mesh, in_specs=placed, out_specs=P("lat", "wave", None, None), check_vma=False
    )
```

```python
import functools

import jax
import jax.numpy as jnp
from jax import lax
from jax.experimental import pallas as pl
from jax.experimental.pallas import tpu as pltpu
from jax.sharding import PartitionSpec as P

MESH = pl.DeviceIdType.MESH
F32 = jnp.float32
BF16 = jnp.bfloat16

MW = 384
NN = 384
NLON = 768
FIELDS = 4
LEVELS = 4
LAYERS = 16
ZH = 4
NY = 8
NX = 4
ZL = 2
R = 8
KW = 48
NI = 6
NB = 128
NA = NLON // NB
JA = 8
JB = 4

QUARTER_SIN = (6.2831854820251465, -41.34168243408203, 81.60247802734375, -76.58128356933594, 39.76072311401367)
QUARTER_COS = (0.9999999403953552, -19.739171981811523, 64.93457794189453, -85.24009704589844, 56.24053955078125)
COS = (1.0, -19.739208221435547, 64.93939208984375, -85.45665740966797, 60.242130279541016, -26.4046688079834,
       7.800131320953369, -1.4531123638153076)
SIN = (6.2831854820251465, -41.34170150756836, 81.6052474975586, -76.70580291748047, 42.05775451660156,
       -15.086565017700195, 3.7813189029693604, -0.6207788586616516)


def iota(shape, dim):
    return lax.broadcasted_iota(jnp.int32, shape, dim)


def split(x):
    hi = x.astype(BF16)
    return hi, (x - hi.astype(F32)).astype(BF16)


def nt(a, b):
    return lax.dot_general(a, b, (((1,), (1,)), ((), ())), preferred_element_type=F32)


def nn(a, b):
    return jnp.dot(a, b, preferred_element_type=F32)


def polynomial(coefficients, u):
    total = jnp.full_like(u, coefficients[-1])
    for c in coefficients[-2::-1]:
        total = total * u + c
    return total


def cos_sin(steps, points, inverse):
    turns = (steps - jnp.floor(steps * inverse + 0.5) * points) * inverse
    u = turns * turns
    return polynomial(COS, u), polynomial(SIN, u) * turns


PIECES = 4


def ring_pieces(extent):
    return [
        (direction, s, q)
        for s in range(extent // 2)
        for late in (0, 1)
        for q in range(PIECES)
        for direction in (0, 1)
        if late == (1 if (q < PIECES // 2) == (direction == 1) else 0) and s >= late
    ]


def chunk_of(extent, direction, s):
    return extent // 2 - s if direction == 0 else extent // 2 + s


def kernel(
    grid_ref, lon_in, order_in, leg_ref, band_in, out_ref,
    lon_ref, order_ref, band_ref, order_row, leg_v, gv, xr, packets, arrived, picked_out, picked_in, xs, fd, ra, rb, ring_a, ring_b, half_a, half_b,
    small_sem, leg_sem, own_sem, leg_send, leg_recv, g_send, g_recv,
    ra_send, ra_recv, rb_send, rb_recv, da_send, da_recv, db_send, db_recv,
):
    lat, wave = lax.axis_index("lat"), lax.axis_index("wave")
    core = lax.rem(lat, 2)
    y = lax.rem(lat // 2, NY)
    zh = lat // (2 * NY)
    x = wave // ZL
    zl = lax.rem(wave, ZL)

    def at_y(o, c):
        return ((zh * NY + lax.rem(y + o + NY, NY)) * 2 + c, wave)

    def at_z(o, c):
        return ((lax.rem(zh + o + ZH, ZH) * NY + y) * 2 + c, wave)

    def wave_at(dx, dz):
        return lax.rem(x + dx, NX) * ZL + lax.rem(zl + dz, ZL)

    def at_w(dx, dz, dc):
        return (lat - core + lax.rem(core + dc, 2), wave_at(dx, dz))

    sibling = (lat + 1 - 2 * core, wave)
    wave_peers = [(dx, dz, dc) for dx in range(NX) for dz in range(ZL) for dc in (0, 1)][1:]
    wave_peers.sort(key=lambda to: -min(to[0], NX - to[0]) - to[1])

    small = [
        pltpu.make_async_copy(source, target, small_sem.at[i])
        for i, (source, target) in enumerate(
            ((lon_in, lon_ref), (order_in, order_row), (order_in, order_ref), (band_in, band_ref))
        )
    ]
    for copy in small:
        copy.start()
    own_copy = pltpu.make_async_copy(grid_ref, gv, own_sem)
    own_copy.start()
    leg_copies = []
    for t in range(NN // NB):
        copy = pltpu.make_async_copy(leg_ref.at[:, t * NB : (t + 1) * NB], leg_v.at[t], leg_sem.at[t])
        copy.start()
        leg_copies.append(copy)
    barrier = pltpu.get_barrier_semaphore()
    both = [at_w(*to) for to in wave_peers]

    def enter(others):
        for peer in both + others:
            pl.semaphore_signal(barrier, inc=1, device_id=peer, device_id_type=MESH)

    z_far, y_far = range(1, ZH), range(1, NY)

    @pl.when(core == 1)
    def _():
        others = [at_y(1, 1), at_y(-1, 1)] + [at_z(o, 1) for o in z_far] + [at_y(o, 0) for o in y_far]
        enter(others)

    @pl.when(core == 0)
    def _():
        others = [at_z(o, 1) for o in z_far] + [at_z(o, 0) for o in z_far] + [at_y(o, 0) for o in y_far]
        enter(others)

    def remote(src, dst, send, recv, peer):
        return pltpu.make_async_remote_copy(
            src_ref=src, dst_ref=dst, send_sem=send, recv_sem=recv, device_id=peer, device_id_type=MESH
        )

    small[0].wait()
    small[1].wait()
    slots = MW
    rows_a_all = 8 * JA * 4
    row = iota((slots, NB), 0)
    in_a = row < rows_a_all
    rest = jnp.where(in_a, row, row - rows_a_all)
    place = (rest // 4) + 8 - wave
    wave_of = jnp.where(in_a, rest // (JA * 4), rest // (JB * 4))
    j_of = jnp.where(in_a, place % JA, JA + place % JB)
    slot_of = wave_of * KW + (rest % 4) * (KW // 4) + j_of
    hit = jnp.concatenate(
        [jnp.where(slot_of == iota((slots, NB), 1) + t * NB, 1.0, 0.0).astype(BF16) for t in range(MW // NB)], axis=1
    )
    hi, lo = split(jnp.broadcast_to(order_row[...].astype(F32)[None, :], (NB, MW)))
    waves = nt(jnp.concatenate([hit, hit], axis=1), jnp.concatenate([hi, lo], axis=1))

    own_copy.wait()
    sub = iota((2 * R, NB), 0)
    points = jnp.zeros((2 * R, NB), jnp.int32)
    for r in range(R):
        points = jnp.where(sub % R == r, lon_ref[r], points)
    column = iota((2 * R, NB), 1)
    for a in range(8):
        if a < NA:
            value = jnp.where(column + a * NB < points, gv[:, a * NB : (a + 1) * NB], 0.0)
        else:
            value = jnp.zeros((2 * R, NB), F32)
        xr[pl.ds(a, 2 * R, stride=8), :] = value

    low = iota((1, NB), 1).astype(F32)
    row_of = (iota((NB, NB), 0) // 8) % R
    first = [None, None]
    for r in range(R):
        inverse = 1.0 / jnp.full((1, NB), lon_ref[r], jnp.int32).astype(F32)
        u = waves * (low * inverse)
        u = u - jnp.floor(u + 0.5)
        v = jnp.abs(u) - 0.25
        square = v * v
        cosine = -v * polynomial(QUARTER_SIN, square)
        sine = polynomial(QUARTER_COS, square)
        minus_sine = jnp.where(u < 0, sine, -sine)
        hi, lo = split(jnp.where(row_of == r, xr[...], 0.0))
        columns = jnp.concatenate([jnp.concatenate([hi, hi], axis=1), jnp.concatenate([lo, lo], axis=1)], axis=0)
        for c, table in enumerate((cosine, minus_sine)):
            part = nt(jnp.concatenate(split(table), axis=1), columns)
            part = part[:, :NB] + part[:, NB:]
            first[c] = part if r == 0 else first[c] + part

    lane = iota((1, NB), 1)
    points = jnp.zeros((1, NB), jnp.int32)
    for r in range(R):
        points = jnp.where((lane // 8) % R == r, lon_ref[r], points)
    points = points.astype(F32)
    high = ((lane % 8) * NB).astype(F32)
    tw_re, tw_im = cos_sin(waves * high, points, 1.0 / points)
    factor = jnp.where(2.0 * waves < points, 1.0 / jnp.sqrt(points), 0.0)
    tw_re, tw_im = tw_re * factor, -tw_im * factor
    re, im = first
    both_parts = jnp.concatenate([re * tw_re - im * tw_im, re * tw_im + im * tw_re], axis=0)
    hi, lo = split(both_parts)
    gather = jnp.where(iota((2 * R, NB), 1) // 8 == iota((2 * R, NB), 0), 1.0, 0.0).astype(BF16)
    spectrum = nt(jnp.concatenate([gather, gather], axis=1), jnp.concatenate([hi, lo], axis=1))

    part_of_a = JA * 4
    for g in range(8):
        for c_to in (0, 1):
            blocks = []
            for layer in (0, 1):
                for c in (0, 1):
                    value = spectrum[layer * R : (layer + 1) * R, c * slots : (c + 1) * slots]
                    if c_to == 1:
                        blocks.append(value[:, g * part_of_a : (g + 1) * part_of_a])
                    else:
                        start = 8 * part_of_a + g * JB * 4
                        blocks += [value[:, start : start + JB * 4]] * 2
            packets[c_to, g] = jnp.concatenate(blocks, axis=1)

    @pl.when(core == 1)
    def _():
        pl.semaphore_wait(barrier, len(both) + 2 + 2 * (ZH - 1))

    @pl.when(core == 0)
    def _():
        pl.semaphore_wait(barrier, len(both) + ZH - 1 + 2 * (NY - 1))

    def packet_copy(i):
        dx, dz, dc = wave_peers[i]
        return remote(
            packets.at[lax.rem(core + dc, 2), wave_at(dx, dz)], arrived.at[core, wave],
            g_send.at[i], g_recv.at[i], at_w(dx, dz, dc),
        )

    for i in range(len(wave_peers)):
        packet_copy(i).start()
    arrived[core, wave] = packets[core, wave]

    n_lane = iota((1, NN), 1).astype(F32) + 0.5
    z_of = jnp.floor(n_lane * (1.0 / (NI * 2 * NY)))
    rest = n_lane - z_of * (NI * 2 * NY)
    y_of = jnp.floor(rest * (1.0 / (NI * 2)))
    rest = rest - y_of * (NI * 2)
    c_of = jnp.floor(rest * (1.0 / NI))
    i_of = rest - c_of * NI - 0.5
    z_rel = z_of - zh.astype(F32)
    z_rel = jnp.where(z_rel < 0, z_rel + ZH, z_rel)
    y_rel = y_of - y.astype(F32)
    y_rel = jnp.where(y_rel < 0, y_rel + NY, y_rel)
    place_a = ((y_rel * ZH + z_rel) * 2 + c_of) * NI + i_of
    place_b = ((z_rel * NY + y_rel) * 2 + c_of) * NI + i_of
    place = jnp.where(core == 1, place_a, place_b)

    def slot(g, q):
        return (q % 4) * (KW // 4) + 2 * g + q // 4

    groups = KW // 8
    cut = JA // 2
    near, far = cut * 8, (groups - cut) * 8
    small[2].wait()
    for copy in leg_copies:
        copy.wait()
    n_of = iota((R, NN), 1)

    def pick(g, q):
        m = order_ref[wave * KW + slot(g, q)]
        picked = jnp.concatenate([leg_v[t, pl.ds(m, R, stride=MW), :] for t in range(NN // NB)], axis=1)
        return jnp.where(n_of >= m, picked, 0.0)

    def rows_copy(c_from):
        count = far if c_from == 1 else near
        return remote(
            picked_out.at[pl.ds(0, count)], picked_in.at[pl.ds(0, count), c_from], leg_send, leg_recv, sibling
        )

    @pl.when(core == 1)
    def _():
        for at in range(far):
            picked_out[at] = pick(cut + at // 8, at % 8)
        rows_copy(1).start()
        for at in range(near):
            picked_in[at, 1] = pick(at // 8, at % 8)

    @pl.when(core == 0)
    def _():
        for at in range(near):
            picked_out[at] = pick(at // 8, at % 8)
        rows_copy(0).start()
        for at in range(far):
            picked_in[at, 0] = pick(cut + at // 8, at % 8)

    order = jnp.where(iota((NN, NN), 0).astype(F32) == place, 1.0, 0.0).astype(BF16)

    def turn_rows(count):
        for g in range(count // 8):
            hi, lo = split(picked_in[g * 8 : (g + 1) * 8].reshape(8 * 2 * R, NN))
            xs[g] = nt(order, jnp.concatenate([hi, lo], axis=0)).astype(BF16)

    lanes = iota((2 * R, NB), 1)
    k4_of = lanes % 4
    place_of = (lanes // 4) % 8
    per_core = 2 * R

    def values_of(j):
        total = jnp.zeros((per_core, NB), F32)
        for g in range(8):
            value = jnp.concatenate([arrived[0, g], arrived[1, g]], axis=0)
            total = jnp.where(place_of == (j + g) % 8, value, total)
        if j == 0:
            return total
        near_roll = pltpu.roll(total, NB - 4 * j, 1)
        far_roll = pltpu.roll(total, 32 - 4 * j, 1)
        return jnp.where(place_of + j < 8, near_roll, far_roll)

    def diagonals(count):
        for g in range(count):
            rows = []
            zero = jnp.zeros((per_core, NB), F32)
            for t in (0, 1):
                value = values_of(2 * g + t)
                for k4 in range(4):
                    one = jnp.where(k4_of == k4, value, 0.0)
                    rows.append(jnp.concatenate([zero, one] if t else [one, zero], axis=1))
            hi, lo = split(jnp.concatenate(rows, axis=0))
            fd[g] = jnp.concatenate([hi, hi, lo], axis=0)

    def chunk_sums(o, count, extent, target, width):
        rows = NN // extent
        for g in range(count):
            turned = xs[g, o * rows : (o + 1) * rows, :]
            sums = nn(turned, fd[g, : 2 * NB, :]) + nn(turned[:, :NB], fd[g, 2 * NB :, :])
            for t in (0, 1):
                target[pl.ds(o * rows * width + 2 * g + t, rows, stride=width), :] = sums[:, t * NB : (t + 1) * NB]

    part_a = NN // NY * JA
    part_b = NN // ZH * JB
    rows_a, rows_b = NI * JA, NI * JB
    y_order = sorted(range(NY), key=lambda o: -min(o, NY - o))
    z_order = sorted(range(ZH), key=lambda o: -min(o, ZH - o))
    def piece_rows(part, o, q):
        return pl.ds(o * part + q * (part // PIECES), part // PIECES)

    def ring_a_copy(direction, s, q):
        return remote(
            ra.at[piece_rows(part_a, chunk_of(NY, direction, s), q)], ring_a.at[direction, s, q],
            ra_send.at[direction, s, q], ra_recv.at[direction, s, q], at_y(1 - 2 * direction, 1),
        )

    def ring_b_copy(direction, s, q):
        return remote(
            rb.at[piece_rows(part_b, chunk_of(ZH, direction, s), q)], ring_b.at[direction, s, q],
            rb_send.at[direction, s, q], rb_recv.at[direction, s, q], at_z(1 - 2 * direction, 0),
        )

    def reduce_ring(extent, part, own, landing, copy, sums, finish):
        every = ring_pieces(extent)

        first = [p for p in every if (p[0], p[1] - 1, p[2]) not in every]
        for o in sorted(range(extent), key=lambda o: -min(o, extent - o)):
            sums(o)
            for p in first:
                if chunk_of(extent, p[0], p[1]) == o:
                    copy(*p).start()
        for p in every:
            if p not in first:
                direction, s, q = p
                rows = piece_rows(part, chunk_of(extent, direction, s), q)
                copy(direction, s - 1, q).wait_recv()
                own[rows, :] = own[rows, :] + landing[direction, s - 1, q]
                copy(*p).start()
        last = extent // 2 - 1
        for q in range(PIECES):
            rows = piece_rows(part, 0, q)
            total = own[rows, :]
            for direction in (0, 1):
                if (direction, last, q) in every:
                    copy(direction, last, q).wait_recv()
                    total = total + landing[direction, last, q]
            own[rows, :] = total
            finish(q)

    def end_a_copy(o, c):
        return remote(
            ra.at[pl.ds((o * 2 + c) * rows_a, rows_a)], half_a.at[pl.ds(o * rows_a, rows_a)],
            da_send.at[o, c], da_recv.at[o], at_z(o, c) if o else sibling,
        )

    def end_b_copy(o, c):
        return remote(
            rb.at[pl.ds((o * 2 + c) * rows_b, rows_b)], half_b.at[pl.ds(o * rows_b, rows_b)],
            db_send.at[o, c], db_recv.at[o], at_y(o, c) if o else sibling,
        )

    end_a = [(o, c) for o in z_order for c in (0, 1) if (o, c) != (0, 1)]
    end_b = [(o, c) for o in y_order for c in (0, 1) if (o, c) != (0, 0)]

    @pl.when(core == 1)
    def _():
        rows_copy(0).wait_recv()
        turn_rows(near)
        for i in range(len(wave_peers)):
            packet_copy(i).wait_recv()
        diagonals(cut)

        def finish(q):
            for o, c in end_a:
                if (o * 2 + c) * rows_a // (part_a // PIECES) == q:
                    end_a_copy(o, c).start()

        reduce_ring(NY, part_a, ra, ring_a, ring_a_copy, lambda o: chunk_sums(o, cut, NY, ra, JA), finish)
        half_a[:rows_a, :] = ra[rows_a : 2 * rows_a, :]
        end_b_copy(0, 1).wait_recv()

    @pl.when(core == 0)
    def _():
        rows_copy(1).wait_recv()
        turn_rows(far)
        for i in range(len(wave_peers)):
            packet_copy(i).wait_recv()
        diagonals(groups - cut)

        def finish(q):
            for o, c in end_b:
                if (o * 2 + c) * rows_b // (part_b // PIECES) == q:
                    end_b_copy(o, c).start()

        reduce_ring(ZH, part_b, rb, ring_b, ring_b_copy, lambda o: chunk_sums(o, groups - cut, ZH, rb, JB), finish)
        half_b[:rows_b, :] = rb[:rows_b, :]
        end_a_copy(0, 0).wait_recv()

    small[3].wait()
    band = [jnp.zeros((1, NB), F32) for _ in range(3)]
    lane = iota((1, NB), 1)
    odd = lane // (NB // 2)
    layer_of = 2 * ((lane // 4) % 8) + odd
    for d in range(3):
        for f in range(FIELDS):
            for l in range(LEVELS):
                if (d, l) in ((0, 0), (2, LEVELS - 1)):
                    continue
                band[d] = jnp.where(layer_of == f * LEVELS + l, band_ref[d, f, l], band[d])

    def vertical(total, width):
        degree = iota(total.shape, 0) // width + lat * NI
        degree = degree.astype(F32)
        ratio = degree * (degree + 1.0) * (1.0 / (MW * MW))
        other = pltpu.roll(total, NB // 2, 1)
        below = jnp.where(odd == 1, other, pltpu.roll(total, NB // 2 + 4, 1))
        above = jnp.where(odd == 0, other, pltpu.roll(total, NB // 2 - 4, 1))
        return total + ratio * (band[0] * below + band[1] * total + band[2] * above)

    total_b = half_b[:rows_b, :]
    for o in y_far:
        end_b_copy(o, 0).wait_recv()
        total_b = total_b + half_b[o * rows_b : (o + 1) * rows_b, :]
    total_b = vertical(total_b, JB)
    total_a = half_a[:rows_a, :]
    for o in z_far:
        end_a_copy(o, 0).wait_recv()
        total_a = total_a + half_a[o * rows_a : (o + 1) * rows_a, :]
    total_a = vertical(total_a, JA)

    total = jnp.concatenate([total_a, total_b], axis=0)
    hi, lo = split(total)
    rest = (total - hi.astype(F32) - lo.astype(F32)).astype(BF16)
    row, lane = iota((NB, NB), 0), iota((NB, NB), 1)
    cl = 2 * LAYERS
    source = (row % 2) * 64 + ((row % cl) // LAYERS) * 32 + ((row % LAYERS) // 2) * 4 + row // cl
    chosen = jnp.where(lane == source, 1.0, 0.0).astype(BF16)
    turned = nt(jnp.concatenate([chosen] * 3, axis=1), jnp.concatenate([hi, lo, rest], axis=1))
    for i in range(NI):
        pieces = []
        for k4 in range(4):
            rows = turned[k4 * cl : (k4 + 1) * cl]
            pieces.append(rows[:, i * JA : (i + 1) * JA])
            pieces.append(rows[:, rows_a + i * JB : rows_a + (i + 1) * JB])
        out_ref[i] = jnp.concatenate(pieces, axis=1)

    for i in range(len(wave_peers)):
        packet_copy(i).wait_send()

    @pl.when(core == 1)
    def _():
        rows_copy(1).wait_send()
        for p in ring_pieces(NY):
            ring_a_copy(*p).wait_send()
        for o, c in end_a:
            end_a_copy(o, c).wait_send()

    @pl.when(core == 0)
    def _():
        rows_copy(0).wait_send()
        for p in ring_pieces(ZH):
            ring_b_copy(*p).wait_send()
        for o, c in end_b:
            end_b_copy(o, c).wait_send()


def shards(grid_field, row_longitudes, owner_order, legendre, vertical_band):
    lw = grid_field.shape[0]
    dma = pltpu.SemaphoreType.DMA
    vmem = pltpu.VMEM
    smem = pltpu.SMEM
    hbm = pl.BlockSpec(memory_space=pltpu.HBM)
    part_a, part_b = NN // NY * JA, NN // ZH * JB
    out = pl.pallas_call(
        kernel,
        out_shape=jax.ShapeDtypeStruct((NI, 2 * LAYERS, KW), F32),
        in_specs=[hbm] * 5,
        out_specs=pl.BlockSpec(memory_space=pltpu.VMEM),
        scratch_shapes=[
            smem((R,), jnp.int32),
            smem((MW,), jnp.int32),
            smem((3, FIELDS, LEVELS), F32),
            vmem((MW,), jnp.int32),
            vmem((NN // NB, R * MW, NB), F32),
            vmem((2 * R, NLON), F32),
            vmem((NB, NB), F32),
            vmem((2, 8, R, NB), F32),
            vmem((2, 8, R, NB), F32),
            vmem((JA * 4, R, NN), F32),
            vmem((JA * 4, 2, R, NN), F32),
            vmem((JA // 2, NN, 2 * NB), BF16),
            vmem((JA // 2, 3 * NB, 2 * NB), BF16),
            vmem((NN * JA, NB), F32),
            vmem((NN * JB, NB), F32),
            vmem((2, NY // 2, PIECES, part_a // PIECES, NB), F32),
            vmem((2, ZH // 2, PIECES, part_b // PIECES, NB), F32),
            vmem((ZH * NI * JA, NB), F32),
            vmem((NY * NI * JB, NB), F32),
            dma((4,)), dma((NN // NB,)), dma, dma, dma,
            dma((2 * NX * ZL - 1,)), dma((2 * NX * ZL - 1,)),
            dma((2, NY // 2, PIECES)), dma((2, NY // 2, PIECES)),
            dma((2, ZH // 2, PIECES)), dma((2, ZH // 2, PIECES)),
            dma((ZH, 2)), dma((ZH,)), dma((NY, 2)), dma((NY,)),
        ],
        compiler_params=pltpu.CompilerParams(
            collective_id=0, has_side_effects=True, vmem_limit_bytes=60 * 1024 * 1024
        ),
    )(
        grid_field.reshape(lw * R, NLON), row_longitudes, owner_order, legendre.reshape(R * MW, NN),
        vertical_band.transpose(1, 0, 2),
    )
    return out.reshape(NI, 2, LAYERS, KW).transpose(0, 3, 1, 2)


def solution(mesh):
    placed = (P("wave", "lat", None), P("lat"), P(), P("lat", None, None), P())
    return jax.shard_map(
        shards, mesh=mesh, in_specs=placed, out_specs=P("lat", "wave", None, None), check_vma=False
    )
```

```python
import functools

import jax
import jax.numpy as jnp
from jax import lax
from jax.experimental import pallas as pl
from jax.experimental.pallas import tpu as pltpu
from jax.sharding import PartitionSpec as P

MESH = pl.DeviceIdType.MESH
F32 = jnp.float32
BF16 = jnp.bfloat16

MW = 384
NN = 384
NLON = 768
FIELDS = 4
LEVELS = 4
LAYERS = 16
ZH = 4
NY = 8
NX = 4
ZL = 2
R = 8
KW = 48
NI = 6
NB = 128
NA = NLON // NB
JA = 8
JB = 4

QUARTER_SIN = (6.2831854820251465, -41.34168243408203, 81.60247802734375, -76.58128356933594, 39.76072311401367)
QUARTER_COS = (0.9999999403953552, -19.739171981811523, 64.93457794189453, -85.24009704589844, 56.24053955078125)
COS = (1.0, -19.739208221435547, 64.93939208984375, -85.45665740966797, 60.242130279541016, -26.4046688079834,
       7.800131320953369, -1.4531123638153076)
SIN = (6.2831854820251465, -41.34170150756836, 81.6052474975586, -76.70580291748047, 42.05775451660156,
       -15.086565017700195, 3.7813189029693604, -0.6207788586616516)


def iota(shape, dim):
    return lax.broadcasted_iota(jnp.int32, shape, dim)


def split(x):
    hi = x.astype(BF16)
    return hi, (x - hi.astype(F32)).astype(BF16)


def nt(a, b):
    return lax.dot_general(a, b, (((1,), (1,)), ((), ())), preferred_element_type=F32)


def nn(a, b):
    return jnp.dot(a, b, preferred_element_type=F32)


def polynomial(coefficients, u):
    total = jnp.full_like(u, coefficients[-1])
    for c in coefficients[-2::-1]:
        total = total * u + c
    return total


def cos_sin(steps, points, inverse):
    turns = (steps - jnp.floor(steps * inverse + 0.5) * points) * inverse
    u = turns * turns
    return polynomial(COS, u), polynomial(SIN, u) * turns


PIECES = 4


def ring_pieces(extent):
    return [
        (direction, s, q)
        for s in range(extent // 2)
        for late in (0, 1)
        for q in range(PIECES)
        for direction in (0, 1)
        if late == (1 if (q < PIECES // 2) == (direction == 1) else 0) and s >= late
    ]


def chunk_of(extent, direction, s):
    return extent // 2 - s if direction == 0 else extent // 2 + s


def kernel(
    grid_ref, lon_in, order_in, leg_ref, band_in, out_ref,
    lon_ref, order_ref, band_ref, order_row, leg_v, gv, xr, packets, arrived, picked_out, picked_in, xs, fd, ra, rb, ring_a, ring_b, half_a, half_b,
    small_sem, leg_sem, own_sem, leg_send, leg_recv, g_send, g_recv,
    ra_send, ra_recv, rb_send, rb_recv, da_send, da_recv, db_send, db_recv,
):
    lat, wave = lax.axis_index("lat"), lax.axis_index("wave")
    core = lax.rem(lat, 2)
    y = lax.rem(lat // 2, NY)
    zh = lat // (2 * NY)
    x = wave // ZL
    zl = lax.rem(wave, ZL)

    def at_y(o, c):
        return ((zh * NY + lax.rem(y + o + NY, NY)) * 2 + c, wave)

    def at_z(o, c):
        return ((lax.rem(zh + o + ZH, ZH) * NY + y) * 2 + c, wave)

    def wave_at(dx, dz):
        return lax.rem(x + dx, NX) * ZL + lax.rem(zl + dz, ZL)

    def at_w(dx, dz, dc):
        return (lat - core + lax.rem(core + dc, 2), wave_at(dx, dz))

    sibling = (lat + 1 - 2 * core, wave)
    wave_peers = [(dx, dz, dc) for dx in range(NX) for dz in range(ZL) for dc in (0, 1)][1:]
    wave_peers.sort(key=lambda to: -min(to[0], NX - to[0]) - to[1])

    small = [
        pltpu.make_async_copy(source, target, small_sem.at[i])
        for i, (source, target) in enumerate(
            ((lon_in, lon_ref), (order_in, order_row), (order_in, order_ref), (band_in, band_ref))
        )
    ]
    for copy in small:
        copy.start()
    own_copy = pltpu.make_async_copy(grid_ref, gv, own_sem)
    own_copy.start()
    leg_copies = []
    for t in range(NN // NB):
        copy = pltpu.make_async_copy(leg_ref.at[:, t * NB : (t + 1) * NB], leg_v.at[t], leg_sem.at[t])
        copy.start()
        leg_copies.append(copy)
    barrier = pltpu.get_barrier_semaphore()
    both = [at_w(*to) for to in wave_peers]

    def enter(others):
        for peer in both + others:
            pl.semaphore_signal(barrier, inc=1, device_id=peer, device_id_type=MESH)

    z_far, y_far = range(1, ZH), range(1, NY)

    @pl.when(core == 1)
    def _():
        others = [at_y(1, 1), at_y(-1, 1)] + [at_z(o, 1) for o in z_far] + [at_y(o, 0) for o in y_far]
        enter(others)

    @pl.when(core == 0)
    def _():
        others = [at_z(o, 1) for o in z_far] + [at_z(o, 0) for o in z_far] + [at_y(o, 0) for o in y_far]
        enter(others)

    def remote(src, dst, send, recv, peer):
        return pltpu.make_async_remote_copy(
            src_ref=src, dst_ref=dst, send_sem=send, recv_sem=recv, device_id=peer, device_id_type=MESH
        )

    small[0].wait()
    small[1].wait()
    slots = MW
    rows_a_all = 8 * JA * 4
    row = iota((slots, NB), 0)
    in_a = row < rows_a_all
    rest = jnp.where(in_a, row, row - rows_a_all)
    place = (rest // 4) + 8 - wave
    wave_of = jnp.where(in_a, rest // (JA * 4), rest // (JB * 4))
    j_of = jnp.where(in_a, place % JA, JA + place % JB)
    slot_of = wave_of * KW + (rest % 4) * (KW // 4) + j_of
    hit = jnp.concatenate(
        [jnp.where(slot_of == iota((slots, NB), 1) + t * NB, 1.0, 0.0).astype(BF16) for t in range(MW // NB)], axis=1
    )
    hi, lo = split(jnp.broadcast_to(order_row[...].astype(F32)[None, :], (NB, MW)))
    waves = nt(jnp.concatenate([hit, hit], axis=1), jnp.concatenate([hi, lo], axis=1))

    own_copy.wait()
    sub = iota((2 * R, NB), 0)
    points = jnp.zeros((2 * R, NB), jnp.int32)
    for r in range(R):
        points = jnp.where(sub % R == r, lon_ref[r], points)
    column = iota((2 * R, NB), 1)
    for a in range(8):
        if a < NA:
            value = jnp.where(column + a * NB < points, gv[:, a * NB : (a + 1) * NB], 0.0)
        else:
            value = jnp.zeros((2 * R, NB), F32)
        xr[pl.ds(a, 2 * R, stride=8), :] = value

    low = iota((1, NB), 1).astype(F32)
    row_of = (iota((NB, NB), 0) // 8) % R
    first = [None, None]
    for r in range(R):
        inverse = 1.0 / jnp.full((1, NB), lon_ref[r], jnp.int32).astype(F32)
        u = waves * (low * inverse)
        u = u - jnp.floor(u + 0.5)
        v = jnp.abs(u) - 0.25
        square = v * v
        cosine = -v * polynomial(QUARTER_SIN, square)
        sine = polynomial(QUARTER_COS, square)
        minus_sine = jnp.where(u < 0, sine, -sine)
        hi, lo = split(jnp.where(row_of == r, xr[...], 0.0))
        columns = jnp.concatenate([jnp.concatenate([hi, hi], axis=1), jnp.concatenate([lo, lo], axis=1)], axis=0)
        for c, table in enumerate((cosine, minus_sine)):
            part = nt(jnp.concatenate(split(table), axis=1), columns)
            part = part[:, :NB] + part[:, NB:]
            first[c] = part if r == 0 else first[c] + part

    lane = iota((1, NB), 1)
    points = jnp.zeros((1, NB), jnp.int32)
    for r in range(R):
        points = jnp.where((lane // 8) % R == r, lon_ref[r], points)
    points = points.astype(F32)
    high = ((lane % 8) * NB).astype(F32)
    tw_re, tw_im = cos_sin(waves * high, points, 1.0 / points)
    factor = jnp.where(2.0 * waves < points, 1.0 / jnp.sqrt(points), 0.0)
    tw_re, tw_im = tw_re * factor, -tw_im * factor
    re, im = first
    both_parts = jnp.concatenate([re * tw_re - im * tw_im, re * tw_im + im * tw_re], axis=0)
    hi, lo = split(both_parts)
    gather = jnp.where(iota((2 * R, NB), 1) // 8 == iota((2 * R, NB), 0), 1.0, 0.0).astype(BF16)
    spectrum = nt(jnp.concatenate([gather, gather], axis=1), jnp.concatenate([hi, lo], axis=1))

    part_of_a = JA * 4
    for g in range(8):
        for c_to in (0, 1):
            blocks = []
            for layer in (0, 1):
                for c in (0, 1):
                    value = spectrum[layer * R : (layer + 1) * R, c * slots : (c + 1) * slots]
                    if c_to == 1:
                        blocks.append(value[:, g * part_of_a : (g + 1) * part_of_a])
                    else:
                        start = 8 * part_of_a + g * JB * 4
                        blocks += [value[:, start : start + JB * 4]] * 2
            packets[c_to, g] = jnp.concatenate(blocks, axis=1)

    @pl.when(core == 1)
    def _():
        pl.semaphore_wait(barrier, len(both) + 2 + 2 * (ZH - 1))

    @pl.when(core == 0)
    def _():
        pl.semaphore_wait(barrier, len(both) + ZH - 1 + 2 * (NY - 1))

    def packet_copy(i):
        dx, dz, dc = wave_peers[i]
        return remote(
            packets.at[lax.rem(core + dc, 2), wave_at(dx, dz)], arrived.at[core, wave],
            g_send.at[i], g_recv.at[i], at_w(dx, dz, dc),
        )

    for i in range(len(wave_peers)):
        packet_copy(i).start()
    arrived[core, wave] = packets[core, wave]

    n_lane = iota((1, NN), 1).astype(F32) + 0.5
    z_of = jnp.floor(n_lane * (1.0 / (NI * 2 * NY)))
    rest = n_lane - z_of * (NI * 2 * NY)
    y_of = jnp.floor(rest * (1.0 / (NI * 2)))
    rest = rest - y_of * (NI * 2)
    c_of = jnp.floor(rest * (1.0 / NI))
    i_of = rest - c_of * NI - 0.5
    z_rel = z_of - zh.astype(F32)
    z_rel = jnp.where(z_rel < 0, z_rel + ZH, z_rel)
    y_rel = y_of - y.astype(F32)
    y_rel = jnp.where(y_rel < 0, y_rel + NY, y_rel)
    place_a = ((y_rel * ZH + z_rel) * 2 + c_of) * NI + i_of
    place_b = ((z_rel * NY + y_rel) * 2 + c_of) * NI + i_of
    place = jnp.where(core == 1, place_a, place_b)

    def slot(g, q):
        return (q % 4) * (KW // 4) + 2 * g + q // 4

    groups = KW // 8
    cut = JA // 2
    near, far = cut * 8, (groups - cut) * 8
    small[2].wait()
    for copy in leg_copies:
        copy.wait()
    n_of = iota((R, NN), 1)

    def pick(g, q):
        m = order_ref[wave * KW + slot(g, q)]
        picked = jnp.concatenate([leg_v[t, pl.ds(m, R, stride=MW), :] for t in range(NN // NB)], axis=1)
        return jnp.where(n_of >= m, picked, 0.0)

    def rows_copy(c_from):
        count = far if c_from == 1 else near
        return remote(
            picked_out.at[pl.ds(0, count)], picked_in.at[pl.ds(0, count), c_from], leg_send, leg_recv, sibling
        )

    @pl.when(core == 1)
    def _():
        for at in range(far):
            picked_out[at] = pick(cut + at // 8, at % 8)
        rows_copy(1).start()
        for at in range(near):
            picked_in[at, 1] = pick(at // 8, at % 8)

    @pl.when(core == 0)
    def _():
        for at in range(near):
            picked_out[at] = pick(at // 8, at % 8)
        rows_copy(0).start()
        for at in range(far):
            picked_in[at, 0] = pick(cut + at // 8, at % 8)

    order = jnp.where(iota((NN, NN), 0).astype(F32) == place, 1.0, 0.0).astype(BF16)

    def turn_rows(count):
        for g in range(count // 8):
            hi, lo = split(picked_in[g * 8 : (g + 1) * 8].reshape(8 * 2 * R, NN))
            xs[g] = nt(order, jnp.concatenate([hi, lo], axis=0)).astype(BF16)

    lanes = iota((2 * R, NB), 1)
    k4_of = lanes % 4
    place_of = (lanes // 4) % 8
    per_core = 2 * R

    def values_of(j):
        total = jnp.zeros((per_core, NB), F32)
        for g in range(8):
            value = jnp.concatenate([arrived[0, g], arrived[1, g]], axis=0)
            total = jnp.where(place_of == (j + g) % 8, value, total)
        if j == 0:
            return total
        near_roll = pltpu.roll(total, NB - 4 * j, 1)
        far_roll = pltpu.roll(total, 32 - 4 * j, 1)
        return jnp.where(place_of + j < 8, near_roll, far_roll)

    def diagonals(count):
        for g in range(count):
            rows = []
            zero = jnp.zeros((per_core, NB), F32)
            for t in (0, 1):
                value = values_of(2 * g + t)
                for k4 in range(4):
                    one = jnp.where(k4_of == k4, value, 0.0)
                    rows.append(jnp.concatenate([zero, one] if t else [one, zero], axis=1))
            hi, lo = split(jnp.concatenate(rows, axis=0))
            fd[g] = jnp.concatenate([hi, hi, lo], axis=0)

    def chunk_sums(o, count, extent, target, width):
        rows = NN // extent
        for g in range(count):
            turned = xs[g, o * rows : (o + 1) * rows, :]
            sums = nn(turned, fd[g, : 2 * NB, :]) + nn(turned[:, :NB], fd[g, 2 * NB :, :])
            for t in (0, 1):
                target[pl.ds(o * rows * width + 2 * g + t, rows, stride=width), :] = sums[:, t * NB : (t + 1) * NB]

    part_a = NN // NY * JA
    part_b = NN // ZH * JB
    rows_a, rows_b = NI * JA, NI * JB
    y_order = sorted(range(NY), key=lambda o: -min(o, NY - o))
    z_order = sorted(range(ZH), key=lambda o: -min(o, ZH - o))
    def piece_rows(part, o, q):
        return pl.ds(o * part + q * (part // PIECES), part // PIECES)

    def ring_a_copy(direction, s, q):
        return remote(
            ra.at[piece_rows(part_a, chunk_of(NY, direction, s), q)], ring_a.at[direction, s, q],
            ra_send.at[direction, s, q], ra_recv.at[direction, s, q], at_y(1 - 2 * direction, 1),
        )

    def ring_b_copy(direction, s, q):
        return remote(
            rb.at[piece_rows(part_b, chunk_of(ZH, direction, s), q)], ring_b.at[direction, s, q],
            rb_send.at[direction, s, q], rb_recv.at[direction, s, q], at_z(1 - 2 * direction, 0),
        )

    def reduce_ring(extent, part, own, landing, copy, sums, finish):
        every = ring_pieces(extent)

        first = [p for p in every if (p[0], p[1] - 1, p[2]) not in every]
        for o in sorted(range(extent), key=lambda o: -min(o, extent - o)):
            sums(o)
            for p in first:
                if chunk_of(extent, p[0], p[1]) == o:
                    copy(*p).start()
        start = {(direction, q): s for direction, s, q in first}
        moved = [p for p in every if p not in first]
        for direction, s, q in sorted(moved, key=lambda p: p[1] - start[p[0], p[2]]):
            rows = piece_rows(part, chunk_of(extent, direction, s), q)
            copy(direction, s - 1, q).wait_recv()
            own[rows, :] = own[rows, :] + landing[direction, s - 1, q]
            copy(direction, s, q).start()
        last = extent // 2 - 1
        for q in sorted(range(PIECES), key=lambda q: abs(2 * q - PIECES)):
            rows = piece_rows(part, 0, q)
            total = own[rows, :]
            for direction in (0, 1):
                if (direction, last, q) in every:
                    copy(direction, last, q).wait_recv()
                    total = total + landing[direction, last, q]
            own[rows, :] = total
            finish(q)

    def end_a_copy(o, c):
        return remote(
            ra.at[pl.ds((o * 2 + c) * rows_a, rows_a)], half_a.at[pl.ds(o * rows_a, rows_a)],
            da_send.at[o, c], da_recv.at[o], at_z(o, c) if o else sibling,
        )

    def end_b_copy(o, c):
        return remote(
            rb.at[pl.ds((o * 2 + c) * rows_b, rows_b)], half_b.at[pl.ds(o * rows_b, rows_b)],
            db_send.at[o, c], db_recv.at[o], at_y(o, c) if o else sibling,
        )

    end_a = [(o, c) for o in z_order for c in (0, 1) if (o, c) != (0, 1)]
    end_b = [(o, c) for o in y_order for c in (0, 1) if (o, c) != (0, 0)]

    @pl.when(core == 1)
    def _():
        rows_copy(0).wait_recv()
        turn_rows(near)
        for i in range(len(wave_peers)):
            packet_copy(i).wait_recv()
        diagonals(cut)

        def finish(q):
            for o, c in end_a:
                if (o * 2 + c) * rows_a // (part_a // PIECES) == q:
                    end_a_copy(o, c).start()

        reduce_ring(NY, part_a, ra, ring_a, ring_a_copy, lambda o: chunk_sums(o, cut, NY, ra, JA), finish)
        half_a[:rows_a, :] = ra[rows_a : 2 * rows_a, :]
        end_b_copy(0, 1).wait_recv()

    @pl.when(core == 0)
    def _():
        rows_copy(1).wait_recv()
        turn_rows(far)
        for i in range(len(wave_peers)):
            packet_copy(i).wait_recv()
        diagonals(groups - cut)

        def finish(q):
            for o, c in end_b:
                if (o * 2 + c) * rows_b // (part_b // PIECES) == q:
                    end_b_copy(o, c).start()

        reduce_ring(ZH, part_b, rb, ring_b, ring_b_copy, lambda o: chunk_sums(o, groups - cut, ZH, rb, JB), finish)
        half_b[:rows_b, :] = rb[:rows_b, :]
        end_a_copy(0, 0).wait_recv()

    small[3].wait()
    band = [jnp.zeros((1, NB), F32) for _ in range(3)]
    lane = iota((1, NB), 1)
    odd = lane // (NB // 2)
    layer_of = 2 * ((lane // 4) % 8) + odd
    for d in range(3):
        for f in range(FIELDS):
            for l in range(LEVELS):
                if (d, l) in ((0, 0), (2, LEVELS - 1)):
                    continue
                band[d] = jnp.where(layer_of == f * LEVELS + l, band_ref[d, f, l], band[d])

    def vertical(total, width):
        degree = iota(total.shape, 0) // width + lat * NI
        degree = degree.astype(F32)
        ratio = degree * (degree + 1.0) * (1.0 / (MW * MW))
        other = pltpu.roll(total, NB // 2, 1)
        below = jnp.where(odd == 1, other, pltpu.roll(total, NB // 2 + 4, 1))
        above = jnp.where(odd == 0, other, pltpu.roll(total, NB // 2 - 4, 1))
        return total + ratio * (band[0] * below + band[1] * total + band[2] * above)

    total_b = half_b[:rows_b, :]
    for o in y_far:
        end_b_copy(o, 0).wait_recv()
        total_b = total_b + half_b[o * rows_b : (o + 1) * rows_b, :]
    total_b = vertical(total_b, JB)
    total_a = half_a[:rows_a, :]
    for o in z_far:
        end_a_copy(o, 0).wait_recv()
        total_a = total_a + half_a[o * rows_a : (o + 1) * rows_a, :]
    total_a = vertical(total_a, JA)

    total = jnp.concatenate([total_a, total_b], axis=0)
    hi, lo = split(total)
    rest = (total - hi.astype(F32) - lo.astype(F32)).astype(BF16)
    row, lane = iota((NB, NB), 0), iota((NB, NB), 1)
    cl = 2 * LAYERS
    source = (row % 2) * 64 + ((row % cl) // LAYERS) * 32 + ((row % LAYERS) // 2) * 4 + row // cl
    chosen = jnp.where(lane == source, 1.0, 0.0).astype(BF16)
    turned = nt(jnp.concatenate([chosen] * 3, axis=1), jnp.concatenate([hi, lo, rest], axis=1))
    for i in range(NI):
        pieces = []
        for k4 in range(4):
            rows = turned[k4 * cl : (k4 + 1) * cl]
            pieces.append(rows[:, i * JA : (i + 1) * JA])
            pieces.append(rows[:, rows_a + i * JB : rows_a + (i + 1) * JB])
        out_ref[i] = jnp.concatenate(pieces, axis=1)

    for i in range(len(wave_peers)):
        packet_copy(i).wait_send()

    @pl.when(core == 1)
    def _():
        rows_copy(1).wait_send()
        for p in ring_pieces(NY):
            ring_a_copy(*p).wait_send()
        for o, c in end_a:
            end_a_copy(o, c).wait_send()

    @pl.when(core == 0)
    def _():
        rows_copy(0).wait_send()
        for p in ring_pieces(ZH):
            ring_b_copy(*p).wait_send()
        for o, c in end_b:
            end_b_copy(o, c).wait_send()


def shards(grid_field, row_longitudes, owner_order, legendre, vertical_band):
    lw = grid_field.shape[0]
    dma = pltpu.SemaphoreType.DMA
    vmem = pltpu.VMEM
    smem = pltpu.SMEM
    hbm = pl.BlockSpec(memory_space=pltpu.HBM)
    part_a, part_b = NN // NY * JA, NN // ZH * JB
    out = pl.pallas_call(
        kernel,
        out_shape=jax.ShapeDtypeStruct((NI, 2 * LAYERS, KW), F32),
        in_specs=[hbm] * 5,
        out_specs=pl.BlockSpec(memory_space=pltpu.VMEM),
        scratch_shapes=[
            smem((R,), jnp.int32),
            smem((MW,), jnp.int32),
            smem((3, FIELDS, LEVELS), F32),
            vmem((MW,), jnp.int32),
            vmem((NN // NB, R * MW, NB), F32),
            vmem((2 * R, NLON), F32),
            vmem((NB, NB), F32),
            vmem((2, 8, R, NB), F32),
            vmem((2, 8, R, NB), F32),
            vmem((JA * 4, R, NN), F32),
            vmem((JA * 4, 2, R, NN), F32),
            vmem((JA // 2, NN, 2 * NB), BF16),
            vmem((JA // 2, 3 * NB, 2 * NB), BF16),
            vmem((NN * JA, NB), F32),
            vmem((NN * JB, NB), F32),
            vmem((2, NY // 2, PIECES, part_a // PIECES, NB), F32),
            vmem((2, ZH // 2, PIECES, part_b // PIECES, NB), F32),
            vmem((ZH * NI * JA, NB), F32),
            vmem((NY * NI * JB, NB), F32),
            dma((4,)), dma((NN // NB,)), dma, dma, dma,
            dma((2 * NX * ZL - 1,)), dma((2 * NX * ZL - 1,)),
            dma((2, NY // 2, PIECES)), dma((2, NY // 2, PIECES)),
            dma((2, ZH // 2, PIECES)), dma((2, ZH // 2, PIECES)),
            dma((ZH, 2)), dma((ZH,)), dma((NY, 2)), dma((NY,)),
        ],
        compiler_params=pltpu.CompilerParams(
            collective_id=0, has_side_effects=True, vmem_limit_bytes=60 * 1024 * 1024
        ),
    )(
        grid_field.reshape(lw * R, NLON), row_longitudes, owner_order, legendre.reshape(R * MW, NN),
        vertical_band.transpose(1, 0, 2),
    )
    return out.reshape(NI, 2, LAYERS, KW).transpose(0, 3, 1, 2)


def solution(mesh):
    placed = (P("wave", "lat", None), P("lat"), P(), P("lat", None, None), P())
    return jax.shard_map(
        shards, mesh=mesh, in_specs=placed, out_specs=P("lat", "wave", None, None), check_vma=False
    )
```

```python
import functools

import jax
import jax.numpy as jnp
from jax import lax
from jax.experimental import pallas as pl
from jax.experimental.pallas import tpu as pltpu
from jax.sharding import PartitionSpec as P

MESH = pl.DeviceIdType.MESH
F32 = jnp.float32
BF16 = jnp.bfloat16

MW = 384
NN = 384
NLON = 768
FIELDS = 4
LEVELS = 4
LAYERS = 16
ZH = 4
NY = 8
NX = 4
ZL = 2
R = 8
KW = 48
NI = 6
NB = 128
NA = NLON // NB
JA = 8
JB = 4

QUARTER_SIN = (6.2831854820251465, -41.34168243408203, 81.60247802734375, -76.58128356933594, 39.76072311401367)
QUARTER_COS = (0.9999999403953552, -19.739171981811523, 64.93457794189453, -85.24009704589844, 56.24053955078125)
COS = (1.0, -19.739208221435547, 64.93939208984375, -85.45665740966797, 60.242130279541016, -26.4046688079834,
       7.800131320953369, -1.4531123638153076)
SIN = (6.2831854820251465, -41.34170150756836, 81.6052474975586, -76.70580291748047, 42.05775451660156,
       -15.086565017700195, 3.7813189029693604, -0.6207788586616516)


def iota(shape, dim):
    return lax.broadcasted_iota(jnp.int32, shape, dim)


def split(x):
    hi = x.astype(BF16)
    return hi, (x - hi.astype(F32)).astype(BF16)


def nt(a, b):
    return lax.dot_general(a, b, (((1,), (1,)), ((), ())), preferred_element_type=F32)


def nn(a, b):
    return jnp.dot(a, b, preferred_element_type=F32)


def polynomial(coefficients, u):
    total = jnp.full_like(u, coefficients[-1])
    for c in coefficients[-2::-1]:
        total = total * u + c
    return total


def cos_sin(steps, points, inverse):
    turns = (steps - jnp.floor(steps * inverse + 0.5) * points) * inverse
    u = turns * turns
    return polynomial(COS, u), polynomial(SIN, u) * turns


PIECES = 4


def ring_pieces(extent):
    return [
        (direction, s, q)
        for s in range(extent // 2)
        for late in (0, 1)
        for q in range(PIECES)
        for direction in (0, 1)
        if late == (1 if (q < PIECES // 2) == (direction == 1) else 0) and s >= late
    ]


def chunk_of(extent, direction, s):
    return extent // 2 - s if direction == 0 else extent // 2 + s


def kernel(
    grid_ref, lon_in, order_in, leg_ref, band_in, out_ref,
    lon_ref, order_ref, band_ref, order_row, leg_v, gv, xr, packets, arrived, picked_out, picked_in, xs, fd, ra, rb, ring_a, ring_b, half_a, half_b,
    small_sem, leg_sem, own_sem, leg_send, leg_recv, g_send, g_recv,
    ra_send, ra_recv, rb_send, rb_recv, da_send, da_recv, db_send, db_recv,
):
    lat, wave = lax.axis_index("lat"), lax.axis_index("wave")
    core = lax.rem(lat, 2)
    y = lax.rem(lat // 2, NY)
    zh = lat // (2 * NY)
    x = wave // ZL
    zl = lax.rem(wave, ZL)

    def at_y(o, c):
        return ((zh * NY + lax.rem(y + o + NY, NY)) * 2 + c, wave)

    def at_z(o, c):
        return ((lax.rem(zh + o + ZH, ZH) * NY + y) * 2 + c, wave)

    def wave_at(dx, dz):
        return lax.rem(x + dx, NX) * ZL + lax.rem(zl + dz, ZL)

    def at_w(dx, dz, dc):
        return (lat - core + lax.rem(core + dc, 2), wave_at(dx, dz))

    sibling = (lat + 1 - 2 * core, wave)
    wave_peers = [(dx, dz, dc) for dx in range(NX) for dz in range(ZL) for dc in (0, 1)][1:]
    wave_peers.sort(key=lambda to: -min(to[0], NX - to[0]) - to[1])

    small = [
        pltpu.make_async_copy(source, target, small_sem.at[i])
        for i, (source, target) in enumerate(
            ((lon_in, lon_ref), (order_in, order_row), (order_in, order_ref), (band_in, band_ref))
        )
    ]
    for copy in small:
        copy.start()
    own_copy = pltpu.make_async_copy(grid_ref, gv, own_sem)
    own_copy.start()
    leg_copies = []
    for t in range(NN // NB):
        copy = pltpu.make_async_copy(leg_ref.at[:, t * NB : (t + 1) * NB], leg_v.at[t], leg_sem.at[t])
        copy.start()
        leg_copies.append(copy)
    barrier = pltpu.get_barrier_semaphore()
    both = [at_w(*to) for to in wave_peers]

    def enter(others):
        for peer in both + others:
            pl.semaphore_signal(barrier, inc=1, device_id=peer, device_id_type=MESH)

    z_far, y_far = range(1, ZH), range(1, NY)

    @pl.when(core == 1)
    def _():
        others = [at_y(1, 1), at_y(-1, 1)] + [at_z(o, 1) for o in z_far] + [at_y(o, 0) for o in y_far]
        enter(others)

    @pl.when(core == 0)
    def _():
        others = [at_z(o, 1) for o in z_far] + [at_z(o, 0) for o in z_far] + [at_y(o, 0) for o in y_far]
        enter(others)

    def remote(src, dst, send, recv, peer):
        return pltpu.make_async_remote_copy(
            src_ref=src, dst_ref=dst, send_sem=send, recv_sem=recv, device_id=peer, device_id_type=MESH
        )

    small[0].wait()
    small[1].wait()
    slots = MW
    rows_a_all = 8 * JA * 4
    row = iota((slots, NB), 0)
    in_a = row < rows_a_all
    rest = jnp.where(in_a, row, row - rows_a_all)
    place = (rest // 4) + 8 - wave
    wave_of = jnp.where(in_a, rest // (JA * 4), rest // (JB * 4))
    j_of = jnp.where(in_a, place % JA, JA + place % JB)
    slot_of = wave_of * KW + (rest % 4) * (KW // 4) + j_of
    hit = jnp.concatenate(
        [jnp.where(slot_of == iota((slots, NB), 1) + t * NB, 1.0, 0.0).astype(BF16) for t in range(MW // NB)], axis=1
    )
    hi, lo = split(jnp.broadcast_to(order_row[...].astype(F32)[None, :], (NB, MW)))
    waves = nt(jnp.concatenate([hit, hit], axis=1), jnp.concatenate([hi, lo], axis=1))

    own_copy.wait()
    sub = iota((2 * R, NB), 0)
    points = jnp.zeros((2 * R, NB), jnp.int32)
    for r in range(R):
        points = jnp.where(sub % R == r, lon_ref[r], points)
    column = iota((2 * R, NB), 1)
    for a in range(8):
        if a < NA:
            value = jnp.where(column + a * NB < points, gv[:, a * NB : (a + 1) * NB], 0.0)
        else:
            value = jnp.zeros((2 * R, NB), F32)
        xr[pl.ds(a, 2 * R, stride=8), :] = value

    low = iota((1, NB), 1).astype(F32)
    row_of = (iota((NB, NB), 0) // 8) % R
    first = [None, None]
    for r in range(R):
        inverse = 1.0 / jnp.full((1, NB), lon_ref[r], jnp.int32).astype(F32)
        u = waves * (low * inverse)
        u = u - jnp.floor(u + 0.5)
        v = jnp.abs(u) - 0.25
        square = v * v
        cosine = -v * polynomial(QUARTER_SIN, square)
        sine = polynomial(QUARTER_COS, square)
        minus_sine = jnp.where(u < 0, sine, -sine)
        hi, lo = split(jnp.where(row_of == r, xr[...], 0.0))
        columns = jnp.concatenate([jnp.concatenate([hi, hi], axis=1), jnp.concatenate([lo, lo], axis=1)], axis=0)
        for c, table in enumerate((cosine, minus_sine)):
            part = nt(jnp.concatenate(split(table), axis=1), columns)
            part = part[:, :NB] + part[:, NB:]
            first[c] = part if r == 0 else first[c] + part

    lane = iota((1, NB), 1)
    points = jnp.zeros((1, NB), jnp.int32)
    for r in range(R):
        points = jnp.where((lane // 8) % R == r, lon_ref[r], points)
    points = points.astype(F32)
    high = ((lane % 8) * NB).astype(F32)
    tw_re, tw_im = cos_sin(waves * high, points, 1.0 / points)
    factor = jnp.where(2.0 * waves < points, 1.0 / jnp.sqrt(points), 0.0)
    tw_re, tw_im = tw_re * factor, -tw_im * factor
    re, im = first
    both_parts = jnp.concatenate([re * tw_re - im * tw_im, re * tw_im + im * tw_re], axis=0)
    hi, lo = split(both_parts)
    gather = jnp.where(iota((2 * R, NB), 1) // 8 == iota((2 * R, NB), 0), 1.0, 0.0).astype(BF16)
    spectrum = nt(jnp.concatenate([gather, gather], axis=1), jnp.concatenate([hi, lo], axis=1))

    part_of_a = JA * 4
    for g in range(8):
        for c_to in (0, 1):
            blocks = []
            for layer in (0, 1):
                for c in (0, 1):
                    value = spectrum[layer * R : (layer + 1) * R, c * slots : (c + 1) * slots]
                    if c_to == 1:
                        blocks.append(value[:, g * part_of_a : (g + 1) * part_of_a])
                    else:
                        start = 8 * part_of_a + g * JB * 4
                        blocks += [value[:, start : start + JB * 4]] * 2
            packets[c_to, g] = jnp.concatenate(blocks, axis=1)

    @pl.when(core == 1)
    def _():
        pl.semaphore_wait(barrier, len(both) + 2 + 2 * (ZH - 1))

    @pl.when(core == 0)
    def _():
        pl.semaphore_wait(barrier, len(both) + ZH - 1 + 2 * (NY - 1))

    def packet_copy(i):
        dx, dz, dc = wave_peers[i]
        return remote(
            packets.at[lax.rem(core + dc, 2), wave_at(dx, dz)], arrived.at[core, wave],
            g_send.at[i], g_recv.at[i], at_w(dx, dz, dc),
        )

    for i in range(len(wave_peers)):
        packet_copy(i).start()
    arrived[core, wave] = packets[core, wave]

    n_lane = iota((1, NN), 1).astype(F32) + 0.5
    z_of = jnp.floor(n_lane * (1.0 / (NI * 2 * NY)))
    rest = n_lane - z_of * (NI * 2 * NY)
    y_of = jnp.floor(rest * (1.0 / (NI * 2)))
    rest = rest - y_of * (NI * 2)
    c_of = jnp.floor(rest * (1.0 / NI))
    i_of = rest - c_of * NI - 0.5
    z_rel = z_of - zh.astype(F32)
    z_rel = jnp.where(z_rel < 0, z_rel + ZH, z_rel)
    y_rel = y_of - y.astype(F32)
    y_rel = jnp.where(y_rel < 0, y_rel + NY, y_rel)
    place_a = ((y_rel * ZH + z_rel) * 2 + c_of) * NI + i_of
    place_b = ((z_rel * NY + y_rel) * 2 + c_of) * NI + i_of
    place = jnp.where(core == 1, place_a, place_b)

    def slot(g, q):
        return (q % 4) * (KW // 4) + 2 * g + q // 4

    groups = KW // 8
    cut = JA // 2
    near, far = cut * 8, (groups - cut) * 8
    small[2].wait()
    for copy in leg_copies:
        copy.wait()
    n_of = iota((R, NN), 1)

    def pick(g, q):
        m = order_ref[wave * KW + slot(g, q)]
        picked = jnp.concatenate([leg_v[t, pl.ds(m, R, stride=MW), :] for t in range(NN // NB)], axis=1)
        return jnp.where(n_of >= m, picked, 0.0)

    def rows_copy(c_from):
        count = far if c_from == 1 else near
        return remote(
            picked_out.at[pl.ds(0, count)], picked_in.at[pl.ds(0, count), c_from], leg_send, leg_recv, sibling
        )

    @pl.when(core == 1)
    def _():
        for at in range(far):
            picked_out[at] = pick(cut + at // 8, at % 8)
        rows_copy(1).start()
        for at in range(near):
            picked_in[at, 1] = pick(at // 8, at % 8)

    @pl.when(core == 0)
    def _():
        for at in range(near):
            picked_out[at] = pick(at // 8, at % 8)
        rows_copy(0).start()
        for at in range(far):
            picked_in[at, 0] = pick(cut + at // 8, at % 8)

    order = jnp.where(iota((NN, NN), 0).astype(F32) == place, 1.0, 0.0).astype(BF16)

    def turn_rows(count):
        for g in range(count // 8):
            hi, lo = split(picked_in[g * 8 : (g + 1) * 8].reshape(8 * 2 * R, NN))
            xs[g] = nt(order, jnp.concatenate([hi, lo], axis=0)).astype(BF16)

    lanes = iota((2 * R, NB), 1)
    k4_of = lanes % 4
    place_of = (lanes // 4) % 8
    per_core = 2 * R

    def values_of(j):
        total = jnp.zeros((per_core, NB), F32)
        for g in range(8):
            value = jnp.concatenate([arrived[0, g], arrived[1, g]], axis=0)
            total = jnp.where(place_of == (j + g) % 8, value, total)
        if j == 0:
            return total
        near_roll = pltpu.roll(total, NB - 4 * j, 1)
        far_roll = pltpu.roll(total, 32 - 4 * j, 1)
        return jnp.where(place_of + j < 8, near_roll, far_roll)

    def diagonals(count):
        for g in range(count):
            rows = []
            zero = jnp.zeros((per_core, NB), F32)
            for t in (0, 1):
                value = values_of(2 * g + t)
                for k4 in range(4):
                    one = jnp.where(k4_of == k4, value, 0.0)
                    rows.append(jnp.concatenate([zero, one] if t else [one, zero], axis=1))
            hi, lo = split(jnp.concatenate(rows, axis=0))
            fd[g] = jnp.concatenate([hi, hi, lo], axis=0)

    def chunk_sums(o, count, extent, target, width):
        rows = NN // extent
        for g in range(count):
            turned = xs[g, o * rows : (o + 1) * rows, :]
            sums = nn(turned, fd[g, : 2 * NB, :]) + nn(turned[:, :NB], fd[g, 2 * NB :, :])
            for t in (0, 1):
                target[pl.ds(o * rows * width + 2 * g + t, rows, stride=width), :] = sums[:, t * NB : (t + 1) * NB]

    part_a = NN // NY * JA
    part_b = NN // ZH * JB
    rows_a, rows_b = NI * JA, NI * JB
    y_order = sorted(range(NY), key=lambda o: -min(o, NY - o))
    z_order = sorted(range(ZH), key=lambda o: -min(o, ZH - o))
    def piece_rows(part, o, q):
        return pl.ds(o * part + q * (part // PIECES), part // PIECES)

    def ring_a_copy(direction, s, q):
        return remote(
            ra.at[piece_rows(part_a, chunk_of(NY, direction, s), q)], ring_a.at[direction, s, q],
            ra_send.at[direction, s, q], ra_recv.at[direction, s, q], at_y(1 - 2 * direction, 1),
        )

    def ring_b_copy(direction, s, q):
        return remote(
            rb.at[piece_rows(part_b, chunk_of(ZH, direction, s), q)], ring_b.at[direction, s, q],
            rb_send.at[direction, s, q], rb_recv.at[direction, s, q], at_z(1 - 2 * direction, 0),
        )

    def reduce_ring(extent, part, own, landing, copy, sums, finish):
        every = ring_pieces(extent)

        first = [p for p in every if (p[0], p[1] - 1, p[2]) not in every]
        for o in sorted(range(extent), key=lambda o: -min(o, extent - o)):
            sums(o)
            for p in first:
                if chunk_of(extent, p[0], p[1]) == o:
                    copy(*p).start()
        start = {(direction, q): s for direction, s, q in first}
        moved = [p for p in every if p not in first]
        for direction, s, q in sorted(moved, key=lambda p: p[1] - start[p[0], p[2]]):
            rows = piece_rows(part, chunk_of(extent, direction, s), q)
            copy(direction, s - 1, q).wait_recv()
            own[rows, :] = own[rows, :] + landing[direction, s - 1, q]
            copy(direction, s, q).start()
        last = extent // 2 - 1
        for q in sorted(range(PIECES), key=lambda q: abs(2 * q - PIECES)):
            rows = piece_rows(part, 0, q)
            total = own[rows, :]
            for direction in (0, 1):
                if (direction, last, q) in every:
                    copy(direction, last, q).wait_recv()
                    total = total + landing[direction, last, q]
            own[rows, :] = total
            finish(q)

    def end_a_copy(o, c):
        return remote(
            ra.at[pl.ds((o * 2 + c) * rows_a, rows_a)], half_a.at[pl.ds(o * rows_a, rows_a)],
            da_send.at[o, c], da_recv.at[o], at_z(o, c) if o else sibling,
        )

    def end_b_copy(o, c):
        return remote(
            rb.at[pl.ds((o * 2 + c) * rows_b, rows_b)], half_b.at[pl.ds(o * rows_b, rows_b)],
            db_send.at[o, c], db_recv.at[o], at_y(o, c) if o else sibling,
        )

    small[3].wait()
    band = [jnp.zeros((1, NB), F32) for _ in range(3)]
    lane = iota((1, NB), 1)
    odd = lane // (NB // 2)
    layer_of = 2 * ((lane // 4) % 8) + odd
    for d in range(3):
        for f in range(FIELDS):
            for l in range(LEVELS):
                if (d, l) in ((0, 0), (2, LEVELS - 1)):
                    continue
                band[d] = jnp.where(layer_of == f * LEVELS + l, band_ref[d, f, l], band[d])

    row, lane_of = iota((NB, NB), 0), iota((NB, NB), 1)
    cl = 2 * LAYERS
    source = (row % 2) * 64 + ((row % cl) // LAYERS) * 32 + ((row % LAYERS) // 2) * 4 + row // cl
    chosen = jnp.where(lane_of == source, 1.0, 0.0).astype(BF16)

    end_a = [(o, c) for o in z_order for c in (0, 1) if (o, c) != (0, 1)]
    end_b = [(o, c) for o in y_order for c in (0, 1) if (o, c) != (0, 0)]

    @pl.when(core == 1)
    def _():
        rows_copy(0).wait_recv()
        turn_rows(near)
        for i in range(len(wave_peers)):
            packet_copy(i).wait_recv()
        diagonals(cut)

        def finish(q):
            for o, c in end_a:
                if (o * 2 + c) * rows_a // (part_a // PIECES) == q:
                    end_a_copy(o, c).start()

        reduce_ring(NY, part_a, ra, ring_a, ring_a_copy, lambda o: chunk_sums(o, cut, NY, ra, JA), finish)
        half_a[:rows_a, :] = ra[rows_a : 2 * rows_a, :]
        end_b_copy(0, 1).wait_recv()

    @pl.when(core == 0)
    def _():
        rows_copy(1).wait_recv()
        turn_rows(far)
        for i in range(len(wave_peers)):
            packet_copy(i).wait_recv()
        diagonals(groups - cut)

        def finish(q):
            for o, c in end_b:
                if (o * 2 + c) * rows_b // (part_b // PIECES) == q:
                    end_b_copy(o, c).start()

        reduce_ring(ZH, part_b, rb, ring_b, ring_b_copy, lambda o: chunk_sums(o, groups - cut, ZH, rb, JB), finish)
        half_b[:rows_b, :] = rb[:rows_b, :]
        end_a_copy(0, 0).wait_recv()

    def vertical(total, width):
        degree = iota(total.shape, 0) // width + lat * NI
        degree = degree.astype(F32)
        ratio = degree * (degree + 1.0) * (1.0 / (MW * MW))
        other = pltpu.roll(total, NB // 2, 1)
        below = jnp.where(odd == 1, other, pltpu.roll(total, NB // 2 + 4, 1))
        above = jnp.where(odd == 0, other, pltpu.roll(total, NB // 2 - 4, 1))
        return total + ratio * (band[0] * below + band[1] * total + band[2] * above)

    total_b = half_b[:rows_b, :]
    for o in y_far:
        end_b_copy(o, 0).wait_recv()
        total_b = total_b + half_b[o * rows_b : (o + 1) * rows_b, :]
    total_b = vertical(total_b, JB)
    total_a = half_a[:rows_a, :]
    for o in z_far:
        end_a_copy(o, 0).wait_recv()
        total_a = total_a + half_a[o * rows_a : (o + 1) * rows_a, :]
    total_a = vertical(total_a, JA)

    total = jnp.concatenate([total_a, total_b], axis=0)
    hi, lo = split(total)
    rest = (total - hi.astype(F32) - lo.astype(F32)).astype(BF16)
    turned = nt(jnp.concatenate([chosen] * 3, axis=1), jnp.concatenate([hi, lo, rest], axis=1))
    for i in range(NI):
        pieces = []
        for k4 in range(4):
            rows = turned[k4 * cl : (k4 + 1) * cl]
            pieces.append(rows[:, i * JA : (i + 1) * JA])
            pieces.append(rows[:, rows_a + i * JB : rows_a + (i + 1) * JB])
        out_ref[i] = jnp.concatenate(pieces, axis=1)

    for i in range(len(wave_peers)):
        packet_copy(i).wait_send()

    @pl.when(core == 1)
    def _():
        rows_copy(1).wait_send()
        for p in ring_pieces(NY):
            ring_a_copy(*p).wait_send()
        for o, c in end_a:
            end_a_copy(o, c).wait_send()

    @pl.when(core == 0)
    def _():
        rows_copy(0).wait_send()
        for p in ring_pieces(ZH):
            ring_b_copy(*p).wait_send()
        for o, c in end_b:
            end_b_copy(o, c).wait_send()


def shards(grid_field, row_longitudes, owner_order, legendre, vertical_band):
    lw = grid_field.shape[0]
    dma = pltpu.SemaphoreType.DMA
    vmem = pltpu.VMEM
    smem = pltpu.SMEM
    hbm = pl.BlockSpec(memory_space=pltpu.HBM)
    part_a, part_b = NN // NY * JA, NN // ZH * JB
    out = pl.pallas_call(
        kernel,
        out_shape=jax.ShapeDtypeStruct((NI, 2 * LAYERS, KW), F32),
        in_specs=[hbm] * 5,
        out_specs=pl.BlockSpec(memory_space=pltpu.VMEM),
        scratch_shapes=[
            smem((R,), jnp.int32),
            smem((MW,), jnp.int32),
            smem((3, FIELDS, LEVELS), F32),
            vmem((MW,), jnp.int32),
            vmem((NN // NB, R * MW, NB), F32),
            vmem((2 * R, NLON), F32),
            vmem((NB, NB), F32),
            vmem((2, 8, R, NB), F32),
            vmem((2, 8, R, NB), F32),
            vmem((JA * 4, R, NN), F32),
            vmem((JA * 4, 2, R, NN), F32),
            vmem((JA // 2, NN, 2 * NB), BF16),
            vmem((JA // 2, 3 * NB, 2 * NB), BF16),
            vmem((NN * JA, NB), F32),
            vmem((NN * JB, NB), F32),
            vmem((2, NY // 2, PIECES, part_a // PIECES, NB), F32),
            vmem((2, ZH // 2, PIECES, part_b // PIECES, NB), F32),
            vmem((ZH * NI * JA, NB), F32),
            vmem((NY * NI * JB, NB), F32),
            dma((4,)), dma((NN // NB,)), dma, dma, dma,
            dma((2 * NX * ZL - 1,)), dma((2 * NX * ZL - 1,)),
            dma((2, NY // 2, PIECES)), dma((2, NY // 2, PIECES)),
            dma((2, ZH // 2, PIECES)), dma((2, ZH // 2, PIECES)),
            dma((ZH, 2)), dma((ZH,)), dma((NY, 2)), dma((NY,)),
        ],
        compiler_params=pltpu.CompilerParams(
            collective_id=0, has_side_effects=True, vmem_limit_bytes=60 * 1024 * 1024
        ),
    )(
        grid_field.reshape(lw * R, NLON), row_longitudes, owner_order, legendre.reshape(R * MW, NN),
        vertical_band.transpose(1, 0, 2),
    )
    return out.reshape(NI, 2, LAYERS, KW).transpose(0, 3, 1, 2)


def solution(mesh):
    placed = (P("wave", "lat", None), P("lat"), P(), P("lat", None, None), P())
    return jax.shard_map(
        shards, mesh=mesh, in_specs=placed, out_specs=P("lat", "wave", None, None), check_vma=False
    )
```
